32 devices in a mesh: ch: 16 (over z, y, core), freq: 2 (over x).
Axes of the slice: x: 2, y: 2, z: 4, core: 2. Of those that a mesh axis runs over, the one named last changes fastest.
Arguments:
- strain: bfloat16 [512, 8, 2048], P('ch'), may hold values from -100 to 100
- channel_ok: int32 [512], P('ch'), may hold values 0 or 1
- window_ok: int32 [512, 8], P('ch'), may hold values 0 or 1
Outputs:
- stack_ahead: bfloat16 [2, 256, 512, 128], P(None, 'freq', 'ch')
- stack_behind: bfloat16 [2, 256, 512, 128], P(None, 'freq', 'ch')
The draws below stay inside these ranges and needn't reach their ends.
All inputs are finite; a program needn't handle non-finite values. No bound on the sum of `channel_ok` or of `window_ok` on one device may be relied on, other than what follows from the above.
Results may differ from the reference program's by a relative error of at most 0.0082.
Values may be sent and summed in bfloat16 or wider, within the bound.
No kernel may reach another device: no remote copies, remote signals or barrier semaphores. Data moves between devices by JAX's collectives and lax.ppermute only.
A program may use at most 64 MiB of HBM per device.

```python
import math
import jax
import jax.numpy as jnp
from jax import lax

WINDOWS = 8
SAMPLES = 2048
BINS = 256
REACH = 128
TIME_HALF = 128
BIN_HALF = 32
CHANNELS = 512


def draw_strain(key, part):
    key_list = jax.random.split(jax.random.fold_in(key, 11), 4)
    segments = SAMPLES // 64
    shape_full = (CHANNELS, WINDOWS, SAMPLES)
    base_noise = jnp.clip(jax.random.normal(key_list[0], shape_full, jnp.float32), -4.0, 4.0)
    channel_gain = jnp.exp(jax.random.uniform(key_list[2], (CHANNELS, 1, 1), jnp.float32, 0.0, math.log(10.0)))
    envelope = jnp.exp(jax.random.uniform(key_list[3], (CHANNELS, WINDOWS, segments), jnp.float32, math.log(0.3), math.log(3.0)))
    result = base_noise * channel_gain * jnp.repeat(envelope, 64, axis=2)
    return jnp.clip(result, -100.0, 100.0).astype(jnp.bfloat16)


def place_ends(values, rng, least, largest):
    longest = values.shape.index(max(values.shape))
    spots = []
    for shift in (0, 1):
        where = [jax.random.randint(jax.random.fold_in(rng, axis), (), 0, length) for axis, length in enumerate(values.shape)]
        where[longest] = (where[longest] + shift) % values.shape[longest]
        spots.append(tuple(where))
    return values.at[spots[0]].set(least).at[spots[1]].set(largest)


def setup_inputs(seed: int = 0) -> dict:
    keys = jax.random.split(jax.random.key(seed), 4)
    strain = draw_strain(jax.random.fold_in(keys[3], 71), 0)
    channel_ok = place_ends((jax.random.randint(keys[1], (CHANNELS,), 0, 8) < 7).astype(jnp.int32), jax.random.fold_in(keys[1], 1), 0, 1)
    window_ok = place_ends((jax.random.randint(keys[2], (CHANNELS, WINDOWS), 0, 4) < 3).astype(jnp.int32), jax.random.fold_in(keys[2], 1), 0, 1)
    return dict(strain=strain, channel_ok=channel_ok, window_ok=window_ok)


def dft_table(first_bin, bin_count):
    bin_freq = first_bin + 1 + jnp.arange(bin_count, dtype=jnp.int32)
    sample_ids = jnp.arange(SAMPLES, dtype=jnp.int32)
    phase = (bin_freq[:, None] * sample_ids[None, :] % SAMPLES).astype(jnp.float32) * (2.0 * math.pi / SAMPLES)
    norm_scale = 1.0 / math.sqrt(SAMPLES)
    return jnp.stack([jnp.cos(phase) * norm_scale, -jnp.sin(phase) * norm_scale], axis=1).astype(jnp.bfloat16)

def reference(strain, channel_ok, window_ok):
    magnitude = jnp.abs(strain.astype(jnp.float32))
    padded = jnp.pad(magnitude, ((0, 0), (0, 0), (TIME_HALF + 1, TIME_HALF)))
    running = jnp.cumsum(padded, axis=2)
    window_sums = running[:, :, 2 * TIME_HALF + 1:] - running[:, :, :SAMPLES]
    level_mean = window_sums / (2 * TIME_HALF + 1)
    leveled = (strain.astype(jnp.float32) / (level_mean + 1e-06)).astype(jnp.bfloat16)
    table_mat = jnp.transpose(dft_table(0, BINS).astype(jnp.float32), (2, 0, 1)).reshape(SAMPLES, 2 * BINS)
    spectra = jnp.dot(leveled.astype(jnp.float32).reshape(CHANNELS * WINDOWS, SAMPLES), table_mat, precision=lax.Precision.HIGHEST, preferred_element_type=jnp.float32)
    spectra = spectra.reshape(CHANNELS, WINDOWS, BINS, 2)
    band_power = spectra[..., 0] * spectra[..., 0] + spectra[..., 1] * spectra[..., 1]
    bin_ids = jnp.arange(BINS, dtype=jnp.int32)
    smoother_ones = (jnp.abs(bin_ids[:, None] - bin_ids[None, :]) <= BIN_HALF).astype(jnp.float32)
    smooth = jnp.dot(band_power.reshape(CHANNELS * WINDOWS, BINS), smoother_ones, precision=lax.Precision.HIGHEST, preferred_element_type=jnp.float32)
    smooth = smooth.reshape(CHANNELS, WINDOWS, BINS) / (2 * BIN_HALF + 1)
    usable = (channel_ok[:, None] * window_ok).astype(jnp.float32)
    white = (spectra * (1.0 / jnp.sqrt(smooth + 1e-06))[..., None] * usable[:, :, None, None]).astype(jnp.bfloat16)
    real_in = jnp.transpose(white[..., 0], (2, 0, 1)).astype(jnp.float32)
    imag_in = jnp.transpose(white[..., 1], (2, 0, 1)).astype(jnp.float32)
    chan_ids = jnp.arange(CHANNELS, dtype=jnp.int32)
    lag_ids = jnp.arange(REACH, dtype=jnp.int32)
    partner_ids = (chan_ids[:, None] + lag_ids[None, :] + 1).astype(jnp.int32)
    back_rows = (chan_ids[:, None] + REACH - 1 - lag_ids[None, :]).astype(jnp.int32)
    back_cols = jnp.broadcast_to(lag_ids[None, :], (CHANNELS, REACH)).astype(jnp.int32)
    usable_pad = jnp.pad(usable, ((0, REACH), (0, 0)))[partner_ids]
    pair_count = lax.optimization_barrier(jnp.sum(usable[:, None, :] * usable_pad, axis=-1))
    divisor = jnp.maximum(pair_count, 1.0)

    def per_bin(inputs):
        real_row, imag_row = inputs
        real_far = jnp.pad(real_row, ((0, REACH), (0, 0)))[partner_ids]
        imag_far = jnp.pad(imag_row, ((0, REACH), (0, 0)))[partner_ids]
        real_sum = lax.optimization_barrier(jnp.sum(real_row[:, None, :] * real_far + imag_row[:, None, :] * imag_far, axis=-1))
        imag_sum = lax.optimization_barrier(jnp.sum(real_row[:, None, :] * imag_far - imag_row[:, None, :] * real_far, axis=-1))
        ahead_re = (real_sum / divisor).astype(jnp.bfloat16)
        ahead_im = (imag_sum / divisor).astype(jnp.bfloat16)
        behind_re = jnp.pad(ahead_re, ((REACH, 0), (0, 0)))[back_rows, back_cols]
        behind_im = -jnp.pad(ahead_im, ((REACH, 0), (0, 0)))[back_rows, back_cols]
        return (jnp.stack([ahead_re, ahead_im]), jnp.stack([behind_re, behind_im]))
    ahead_all, behind_all = lax.map(per_bin, (real_in, imag_in))
    return (jnp.transpose(ahead_all, (1, 0, 2, 3)), jnp.transpose(behind_all, (1, 0, 2, 3)))
```

```python
import functools
import math

import jax
import jax.numpy as jnp
import ml_dtypes
import numpy as np
from jax import lax
from jax.experimental import pallas as pl
from jax.experimental.pallas import tpu as pltpu
from jax.sharding import PartitionSpec as P

WINDOWS = 8
BINS = 256
REACH = 128
TIME_HALF = 128
BIN_HALF = 32
LANES = 128
PACK = LANES // (2 * WINDOWS)
STEP = 2
VMEM_BYTES = 40 * 1024 * 1024


def bin_columns(bin_count):
    halo = np.concatenate([np.arange(-BIN_HALF, 0), np.arange(bin_count, bin_count + BIN_HALF)])
    own = np.arange(bin_count).reshape(-1, 1, PACK)
    parts = np.arange(2).reshape(1, 2, 1)
    shape = (bin_count // PACK, 2, PACK)
    bins = np.concatenate([halo, halo, np.broadcast_to(own, shape).ravel()])
    part = np.concatenate(
        [np.zeros_like(halo), np.ones_like(halo), np.broadcast_to(parts, shape).ravel()]
    )
    return bins, part


def dft_tables(freq_devices, samples):
    bin_count = BINS // freq_devices
    bins, part = bin_columns(bin_count)
    sample_ids = np.arange(samples)
    tables = []
    for device in range(freq_devices):
        freq = device * bin_count + bins + 1
        inside = (freq >= 1) & (freq <= BINS)
        turn = (freq[None, :] * sample_ids[:, None]) % samples
        phase = turn.astype(np.float32) * np.float32(2.0 * math.pi / samples)
        wave = np.where(part[None, :] == 0, np.cos(phase), -np.sin(phase)).astype(np.float32)
        wave = wave * np.float32(1.0 / math.sqrt(samples)) * inside[None, :]
        tables.append(wave.astype(ml_dtypes.bfloat16))
    return np.stack(tables)


def smoother(bin_count):
    bins, _ = bin_columns(bin_count)
    own = bins[4 * BIN_HALF :]
    return (np.abs(bins[:, None] - own[None, :]) <= BIN_HALF).astype(ml_dtypes.bfloat16)


def whiten_kernel(x_ref, ok_ref, win_ref, table_ref, smooth_ref, out_ref, mag_ref, spec_ref):
    channels, windows, samples = x_ref.shape
    rows = channels * windows
    halo = 4 * BIN_HALF
    own = table_ref.shape[1] - halo
    tile = 2 * TIME_HALF
    count = 2 * TIME_HALF + 1

    mag_ref[:, :TIME_HALF] = jnp.zeros((rows, TIME_HALF), jnp.bfloat16)
    mag_ref[:, TIME_HALF + samples :] = jnp.zeros((rows, TIME_HALF), jnp.bfloat16)
    for t in range(samples // tile):
        x = x_ref[:, :, t * tile : (t + 1) * tile].astype(jnp.float32).reshape(rows, tile)
        mag_ref[:, TIME_HALF + t * tile : TIME_HALF + (t + 1) * tile] = jnp.abs(x).astype(
            jnp.bfloat16
        )
    source = lax.broadcasted_iota(jnp.int32, (2 * tile, tile), 0) - TIME_HALF
    target = lax.broadcasted_iota(jnp.int32, (2 * tile, tile), 1)
    band = (jnp.abs(source - target) <= TIME_HALF).astype(jnp.float32).astype(jnp.bfloat16)
    spectra = jnp.zeros((rows, own + halo), jnp.float32)
    for t in range(samples // tile):
        sums = jnp.dot(
            mag_ref[:, t * tile : (t + 2) * tile], band, preferred_element_type=jnp.float32
        )
        x = x_ref[:, :, t * tile : (t + 1) * tile].astype(jnp.float32).reshape(rows, tile)
        leveled = (x * (count / (sums + count * 1e-06))).astype(jnp.bfloat16)
        spectra = spectra + jnp.dot(
            leveled, table_ref[t * tile : (t + 1) * tile, :], preferred_element_type=jnp.float32
        )

    power = spectra * spectra
    high = power.astype(jnp.bfloat16)
    low = (power - high.astype(jnp.float32)).astype(jnp.bfloat16)
    ones = smooth_ref[...]
    smooth = jnp.dot(high, ones, preferred_element_type=jnp.float32) + jnp.dot(
        low, ones, preferred_element_type=jnp.float32
    )
    white = spectra[:, halo:] * lax.rsqrt(smooth * (1.0 / (2 * BIN_HALF + 1)) + 1e-06)
    for t in range(0, own, LANES):
        width = min(LANES, own - t)
        spec_ref[t // LANES, :, :width] = white[:, t : t + width]

    flags = (ok_ref[...] * win_ref[...]).astype(jnp.float32).astype(jnp.bfloat16)
    lane = lax.broadcasted_iota(jnp.int32, (windows, LANES), 1)
    window = lax.broadcasted_iota(jnp.int32, (windows, LANES), 0)
    contract = (((0,), (0,)), ((), ()))
    picked = (lane == window).astype(jnp.float32).astype(jnp.bfloat16)
    out_ref[:, windows * own :] = lax.dot_general(
        flags, picked, contract, preferred_element_type=jnp.float32
    ).astype(jnp.bfloat16)
    spread = (lane // (2 * PACK) == window).astype(jnp.float32).astype(jnp.bfloat16)
    usable = lax.dot_general(flags, spread, contract, preferred_element_type=jnp.float32)

    width = 2 * PACK
    for g in range(own // width):
        pieces = [
            spec_ref[g * width // LANES, pl.ds(w, channels, stride=windows), :][
                :, g * width % LANES : g * width % LANES + width
            ]
            for w in range(windows)
        ]
        packed = jnp.concatenate(pieces, axis=1) * usable
        out_ref[:, g * LANES : (g + 1) * LANES] = packed.astype(jnp.bfloat16)


def whiten(strain, channel_ok, window_ok, freq_devices):
    channels, windows, samples = strain.shape
    bin_count = BINS // freq_devices
    tables = jnp.asarray(dft_tables(freq_devices, samples))
    ones = jnp.asarray(smoother(bin_count))
    columns = tables.shape[2]
    own = 2 * bin_count
    whole = lambda *shape: pl.BlockSpec(shape, lambda i, q: (0,) * len(shape))
    return pl.pallas_call(
        lambda q_ref, *refs: whiten_kernel(*refs),
        grid_spec=pltpu.PrefetchScalarGridSpec(
            num_scalar_prefetch=1,
            grid=(1,),
            in_specs=[
                whole(channels, windows, samples),
                whole(1, channels),
                whole(windows, channels),
                pl.BlockSpec((None, samples, columns), lambda i, q: (q[0], 0, 0)),
                whole(columns, own),
            ],
            out_specs=whole(channels, windows * own + LANES),
            scratch_shapes=[
                pltpu.VMEM((channels * windows, samples + 2 * TIME_HALF), jnp.bfloat16),
                pltpu.VMEM((-(-own // LANES), channels * windows, LANES), jnp.float32),
            ],
        ),
        out_shape=jax.ShapeDtypeStruct((channels, windows * own + LANES), jnp.bfloat16),
        compiler_params=pltpu.CompilerParams(vmem_limit_bytes=VMEM_BYTES),
        name="whiten",
    )(
        lax.axis_index("freq").reshape(1).astype(jnp.int32),
        strain,
        channel_ok.reshape(1, channels),
        window_ok.T,
        tables,
        ones,
    )


def trade(value, partner):
    count = lax.axis_size("ch")
    pairs = [(i, partner(i)) for i in range(count) if 0 <= partner(i) < count]
    return lax.ppermute(value, "ch", pairs)


def beside(i):
    return i ^ 1


def near(i):
    k, core = i // 2, i % 2
    step = 1 - 2 * ((k + core) % 2)
    return 2 * (k + step) + core


def far(i):
    k, core = i // 2, i % 2
    step = 2 - 4 * ((k // 2 + core) % 2)
    return 2 * (k + step) + core


def cross_kernel(
    own_ref, mate_ref, near_ref, far_ref, near2_ref, far2_ref,
    own_u, mate_u, near_u, far_u, near2_u, far2_u,
    ahead_ref, behind_ref, div_ahead, div_behind,
):
    channels = own_ref.shape[0]
    index = lax.axis_index("ch")
    core = lax.rem(index, 2)
    pair = index // 2
    near_up = lax.rem(pair + core, 2) == 0
    far_up = lax.rem(pair // 2 + core, 2) == 0
    first = core == 0

    def neighbours(own, mate, near, far, near2, far2):
        def ordered(mine, theirs, up):
            block = jnp.where(up, mine, theirs)
            low, high = block[:channels], block[channels:]
            keep = first == up
            return jnp.where(keep, low, high), jnp.where(keep, high, low)

        up1 = ordered(near, near2, near_up)
        down1 = ordered(near, near2, jnp.logical_not(near_up))
        up2 = ordered(far, far2, far_up)
        down2 = ordered(far, far2, jnp.logical_not(far_up))
        pick = lambda a, b: jnp.where(first, a, b)
        ahead = [own, pick(mate, up1[0]), pick(up1[0], up1[1]), pick(up1[1], up2[0]), pick(up2[0], up2[1])]
        behind = [pick(down2[0], down2[1]), pick(down2[1], down1[0]), pick(down1[0], down1[1]), pick(down1[1], mate), own]
        return jnp.concatenate(ahead, axis=0), jnp.concatenate(behind, axis=0)

    total = REACH + channels
    fold = lax.broadcasted_iota(jnp.int32, (total, total), 0)
    source = lax.broadcasted_iota(jnp.int32, (total, total), 1)
    lead = 2 * channels - 1
    wanted = jnp.where(
        fold < channels,
        lead - fold,
        jnp.where(fold < REACH, REACH + lead - fold, REACH + channels - 1 - fold),
    )
    turn = (wanted == source).astype(jnp.float32).astype(jnp.bfloat16)

    def arranged(rows_ahead, rows_behind):
        turned = jnp.dot(turn, rows_behind, preferred_element_type=jnp.float32).astype(jnp.bfloat16)
        return jnp.concatenate(
            [rows_ahead[:REACH], turned[:REACH], rows_ahead[REACH:], turned[REACH:]], axis=0
        )

    row = lax.broadcasted_iota(jnp.int32, (channels, LANES), 0)
    lane = lax.broadcasted_iota(jnp.int32, (channels, LANES), 1)
    wrap_ahead = lane <= row
    wrap_behind = (lane >= channels) & (lane <= lead - row)
    flip = 7 - lax.broadcasted_iota(jnp.int32, (8, LANES), 0)

    def turned_rows(v):
        return jnp.take_along_axis(v, flip, axis=0)

    def skewed(product):
        ends = jnp.concatenate(
            [product[:, 2 * REACH :], jnp.zeros((channels, REACH - 2 * channels), jnp.float32)], axis=1
        )
        a = jnp.where(wrap_ahead, ends, product[:, :REACH])
        b = jnp.where(wrap_behind, ends, product[:, REACH : 2 * REACH])
        aheads = []
        for r in range(0, channels, 8):
            v = pltpu.roll(turned_rows(a[r : r + 8]), (2 * LANES - r - 8) % LANES, 1, stride=1, stride_axis=0)
            aheads.append(turned_rows(v))
        b = pltpu.roll(b, 2 * LANES - 2 * channels - LANES, 1, stride=1, stride_axis=0)
        return jnp.concatenate(aheads, axis=0), b

    contract = (((1,), (1,)), ((), ()))

    @pl.when(pl.program_id(0) == 0)
    def _():
        rhs = arranged(*neighbours(*(r[...] for r in (own_u, mate_u, near_u, far_u, near2_u, far2_u))))
        counts = lax.dot_general(own_u[...], rhs, contract, preferred_element_type=jnp.float32)
        ahead, behind = skewed(counts)
        div_ahead[...] = 1.0 / jnp.maximum(ahead, 1.0)
        div_behind[...] = 1.0 / jnp.maximum(behind, 1.0)

    rows_ahead, rows_behind = neighbours(
        *(r[...] for r in (own_ref, mate_ref, near_ref, far_ref, near2_ref, far2_ref))
    )
    rhs = arranged(rows_ahead, rows_behind)
    for s in range(STEP):
        lanes = slice(s * LANES, (s + 1) * LANES)
        a = own_ref[:, lanes].astype(jnp.float32)
        part = lax.rem(lane // PACK, 2)
        rotated = jnp.where(part == 0, -pltpu.roll(a, LANES - PACK, 1), pltpu.roll(a, PACK, 1))
        zero = jnp.zeros_like(a)
        rows = []
        for f in range(PACK):
            mask = lax.rem(lane, PACK) == f
            rows += [jnp.where(mask, a, zero), jnp.where(mask, rotated, zero)]
        lhs = jnp.concatenate(rows, axis=0).astype(jnp.bfloat16)
        product = lax.dot_general(lhs, rhs[:, lanes], contract, preferred_element_type=jnp.float32)
        for f in range(PACK):
            for v in range(2):
                start = (2 * f + v) * channels
                ahead, behind = skewed(product[start : start + channels])
                ahead_ref[v, s * PACK + f] = (ahead * div_ahead[...]).astype(jnp.bfloat16)
                behind_ref[v, s * PACK + f] = (behind * div_behind[...]).astype(jnp.bfloat16)


def cross(own, mate, near_rows, far_rows, near2, far2, bin_count):
    channels = own.shape[0]
    width = STEP * LANES
    usable_at = bin_count // PACK
    values = [own, mate, near_rows, far_rows, near2, far2]
    specs = [pl.BlockSpec((v.shape[0], width), lambda g: (0, g)) for v in values]
    flags = [pl.BlockSpec((v.shape[0], LANES), lambda g: (0, usable_at)) for v in values]
    out = pl.BlockSpec((2, STEP * PACK, channels, REACH), lambda g: (0, g, 0, 0))
    shape = jax.ShapeDtypeStruct((2, bin_count, channels, REACH), jnp.bfloat16)
    return pl.pallas_call(
        cross_kernel,
        grid=(bin_count // (STEP * PACK),),
        in_specs=specs + flags,
        out_specs=[out, out],
        out_shape=[shape, shape],
        scratch_shapes=[pltpu.VMEM((channels, REACH), jnp.float32)] * 2,
        compiler_params=pltpu.CompilerParams(vmem_limit_bytes=VMEM_BYTES),
        name="cross",
    )(*values, *values)


def per_device(strain, channel_ok, window_ok):
    freq_devices = lax.axis_size("freq")
    own = whiten(strain, channel_ok, window_ok, freq_devices)
    mate = trade(own, beside)
    both = jnp.concatenate([own, mate], axis=0)
    near_rows = trade(both, near)
    far_rows = trade(both, far)
    near2 = trade(near_rows, beside)
    far2 = trade(far_rows, beside)
    return cross(own, mate, near_rows, far_rows, near2, far2, BINS // freq_devices)


def solution(mesh):
    return jax.shard_map(
        per_device,
        mesh=mesh,
        in_specs=(P("ch", None, None), P("ch"), P("ch", None)),
        out_specs=(P(None, "freq", "ch", None), P(None, "freq", "ch", None)),
        check_vma=False,
    )
```

```python
import functools
import math

import jax
import jax.numpy as jnp
import ml_dtypes
import numpy as np
from jax import lax
from jax.experimental import pallas as pl
from jax.experimental.pallas import tpu as pltpu
from jax.sharding import PartitionSpec as P

WINDOWS = 8
BINS = 256
REACH = 128
TIME_HALF = 128
BIN_HALF = 32
LANES = 128
PACK = LANES // (2 * WINDOWS)
CHUNK = 2048
WIDE = 512
VMEM_BYTES = 40 * 1024 * 1024


def bin_columns(bin_count):
    halo = np.concatenate([np.arange(-BIN_HALF, 0), np.arange(bin_count, bin_count + BIN_HALF)])
    own = np.arange(bin_count).reshape(-1, 1, PACK)
    parts = np.arange(2).reshape(1, 2, 1)
    shape = (bin_count // PACK, 2, PACK)
    bins = np.concatenate([halo, halo, np.broadcast_to(own, shape).ravel()])
    part = np.concatenate(
        [np.zeros_like(halo), np.ones_like(halo), np.broadcast_to(parts, shape).ravel()]
    )
    return bins, part


def dft_tables(freq_devices, samples):
    bin_count = BINS // freq_devices
    bins, part = bin_columns(bin_count)
    sample_ids = np.arange(samples)
    tables = []
    for device in range(freq_devices):
        freq = device * bin_count + bins + 1
        inside = (freq >= 1) & (freq <= BINS)
        turn = (freq[None, :] * sample_ids[:, None]) % samples
        phase = turn.astype(np.float32) * np.float32(2.0 * math.pi / samples)
        wave = np.where(part[None, :] == 0, np.cos(phase), -np.sin(phase)).astype(np.float32)
        wave = wave * np.float32(1.0 / math.sqrt(samples)) * inside[None, :]
        tables.append(wave.astype(ml_dtypes.bfloat16))
    return np.stack(tables)


def smoother(bin_count):
    bins, _ = bin_columns(bin_count)
    own = bins[4 * BIN_HALF :]
    return (np.abs(bins[:, None] - own[None, :]) <= BIN_HALF).astype(ml_dtypes.bfloat16)


def whiten_kernel(
    x_hbm, ok_hbm, win_hbm, table_hbm, smooth_hbm, out_ref,
    x_ref, ok_ref, win_ref, table_ref, smooth_ref, mag_ref, level_ref, spec_ref, x_sems, table_sems, sems,
):
    channels, windows, samples = x_ref.shape
    rows = channels * windows
    halo = 4 * BIN_HALF
    own = table_ref.shape[1] - halo
    tile = 2 * TIME_HALF
    count = 2 * TIME_HALF + 1
    tiles = samples // tile
    q = lax.axis_index("freq")

    def chunk(k):
        return pl.ds(k * CHUNK, CHUNK)

    x_copies = [
        pltpu.make_async_copy(x_hbm.at[:, :, chunk(k)], x_ref.at[:, :, chunk(k)], x_sems.at[k])
        for k in range(samples // CHUNK)
    ]
    table_copies = [
        pltpu.make_async_copy(table_hbm.at[q, chunk(k)], table_ref.at[chunk(k)], table_sems.at[k])
        for k in range(samples // CHUNK)
    ]
    small_copies = [
        pltpu.make_async_copy(source, target, sems.at[k])
        for k, (source, target) in enumerate(
            ((ok_hbm, ok_ref), (win_hbm, win_ref), (smooth_hbm, smooth_ref))
        )
    ]
    for copy in x_copies + table_copies + small_copies:
        copy.start()

    mag_ref[:, :TIME_HALF] = jnp.zeros((rows, TIME_HALF), jnp.bfloat16)
    mag_ref[:, TIME_HALF + samples :] = jnp.zeros((rows, TIME_HALF), jnp.bfloat16)
    source = lax.broadcasted_iota(jnp.int32, (2 * tile, tile), 0) - TIME_HALF
    target = lax.broadcasted_iota(jnp.int32, (2 * tile, tile), 1)
    band = (jnp.abs(source - target) <= TIME_HALF).astype(jnp.float32).astype(jnp.bfloat16)

    def loaded(t):
        return x_ref[:, :, t * tile : (t + 1) * tile].astype(jnp.float32).reshape(rows, tile)

    for t in range(tiles):
        if t * tile % CHUNK == 0:
            x_copies[t * tile // CHUNK].wait()
        mag_ref[:, TIME_HALF + t * tile : TIME_HALF + (t + 1) * tile] = jnp.abs(loaded(t)).astype(
            jnp.bfloat16
        )
    for t in range(tiles):
        sums = jnp.dot(
            mag_ref[:, t * tile : (t + 2) * tile], band, preferred_element_type=jnp.float32
        )
        level_ref[:, t * tile : (t + 1) * tile] = (
            loaded(t) * (count / (sums + count * 1e-06))
        ).astype(jnp.bfloat16)
    for copy in table_copies + small_copies:
        copy.wait()
    spectra = jnp.dot(level_ref[...], table_ref[...], preferred_element_type=jnp.float32)

    power = spectra * spectra
    high = power.astype(jnp.bfloat16)
    low = (power - high.astype(jnp.float32)).astype(jnp.bfloat16)
    ones = smooth_ref[...]
    smooth = jnp.dot(high, ones, preferred_element_type=jnp.float32) + jnp.dot(
        low, ones, preferred_element_type=jnp.float32
    )
    white = spectra[:, halo:] * lax.rsqrt(smooth * (1.0 / (2 * BIN_HALF + 1)) + 1e-06)
    for t in range(0, own, LANES):
        width = min(LANES, own - t)
        spec_ref[t // LANES, :, :width] = white[:, t : t + width]

    flags = (ok_ref[...] * win_ref[...]).astype(jnp.float32).astype(jnp.bfloat16)
    lane = lax.broadcasted_iota(jnp.int32, (windows, LANES), 1)
    window = lax.broadcasted_iota(jnp.int32, (windows, LANES), 0)
    contract = (((0,), (0,)), ((), ()))
    picked = (lane == window).astype(jnp.float32).astype(jnp.bfloat16)
    out_ref[:, windows * own :] = lax.dot_general(
        flags, picked, contract, preferred_element_type=jnp.float32
    ).astype(jnp.bfloat16)
    spread = (lane // (2 * PACK) == window).astype(jnp.float32).astype(jnp.bfloat16)
    usable = lax.dot_general(flags, spread, contract, preferred_element_type=jnp.float32)

    width = 2 * PACK
    for g in range(own // width):
        pieces = [
            spec_ref[g * width // LANES, pl.ds(w, channels, stride=windows), :][
                :, g * width % LANES : g * width % LANES + width
            ]
            for w in range(windows)
        ]
        packed = jnp.concatenate(pieces, axis=1) * usable
        out_ref[:, g * LANES : (g + 1) * LANES] = packed.astype(jnp.bfloat16)


def whiten(strain, channel_ok, window_ok, freq_devices):
    channels, windows, samples = strain.shape
    bin_count = BINS // freq_devices
    tables = jnp.asarray(dft_tables(freq_devices, samples))
    ones = jnp.asarray(smoother(bin_count))
    columns = tables.shape[2]
    own = 2 * bin_count
    rows = channels * windows
    chunks = samples // CHUNK
    return pl.pallas_call(
        whiten_kernel,
        in_specs=[pl.BlockSpec(memory_space=pltpu.HBM)] * 5,
        out_specs=pl.BlockSpec(memory_space=pltpu.VMEM),
        out_shape=pltpu.VMEM((channels, windows * own + LANES), jnp.bfloat16),
        scratch_shapes=[
            pltpu.VMEM((channels, windows, samples), jnp.bfloat16),
            pltpu.VMEM((1, channels), jnp.int32),
            pltpu.VMEM((windows, channels), jnp.int32),
            pltpu.VMEM((samples, columns), jnp.bfloat16),
            pltpu.VMEM((columns, own), jnp.bfloat16),
            pltpu.VMEM((rows, samples + 2 * TIME_HALF), jnp.bfloat16),
            pltpu.VMEM((rows, samples), jnp.bfloat16),
            pltpu.VMEM((-(-own // LANES), rows, LANES), jnp.float32),
            pltpu.SemaphoreType.DMA((chunks,)),
            pltpu.SemaphoreType.DMA((chunks,)),
            pltpu.SemaphoreType.DMA((3,)),
        ],
        compiler_params=pltpu.CompilerParams(vmem_limit_bytes=VMEM_BYTES),
        name="whiten",
    )(
        *(
            pltpu.with_memory_space_constraint(value, pltpu.HBM)
            for value in (strain, channel_ok.reshape(1, channels), window_ok.T, tables, ones)
        )
    )


def trade(value, partner):
    count = lax.axis_size("ch")
    pairs = [(i, partner(i)) for i in range(count) if 0 <= partner(i) < count]
    return lax.ppermute(value, "ch", pairs)


def beside(i):
    return i ^ 1


def partner_pair(i):
    return i ^ 2


def other_pair(i):
    return i + 2 if i // 2 % 2 else i - 2


def partner_far(i):
    return i ^ 4


def other_far(i):
    return i + 4 if i // 4 % 2 else i - 4


def cross_kernel(order, own_ref, mate_ref, *refs):
    arrived = [refs[at + order.index(k)] for at in (0, 4) for k in range(4)]
    (ahead_hbm, behind_hbm, partners_ref, div_ahead, div_behind, *products) = refs[8:-3]
    ahead_ref, behind_ref, sems = refs[-3:]
    channels = own_ref.shape[0]
    packs = own_ref.shape[1] // LANES - 1
    index = lax.axis_index("ch")
    first = lax.rem(index, 2) == 0
    pair = index // 2
    near_up = lax.rem(pair, 2) == 0
    far_up = lax.rem(pair // 2, 2) == 0

    def neighbours(lanes):
        pick = lambda a, b: jnp.where(first, a, b)
        own, mate = own_ref[:, lanes], mate_ref[:, lanes]
        mine, theirs = [r[:, lanes] for r in arrived[:4]], [r[:, lanes] for r in arrived[4:]]
        met = [(pick(a, b), pick(b, a)) for a, b in zip(mine, theirs, strict=True)]
        choose = lambda up, a, b: tuple(jnp.where(up, x, y) for x, y in zip(a, b, strict=True))
        up1, down1 = choose(near_up, met[0], met[1]), choose(near_up, met[1], met[0])
        up2, down2 = choose(far_up, met[2], met[3]), choose(far_up, met[3], met[2])
        ahead = [own, pick(mate, up1[0]), pick(up1[0], up1[1]), pick(up1[1], up2[0]), pick(up2[0], up2[1])]
        behind = [pick(down2[0], down2[1]), pick(down2[1], down1[0]), pick(down1[0], down1[1]), pick(down1[1], mate), own]
        return jnp.concatenate(ahead, axis=0), jnp.concatenate(behind, axis=0)

    total = REACH + channels
    fold = lax.broadcasted_iota(jnp.int32, (total, total), 0)
    source = lax.broadcasted_iota(jnp.int32, (total, total), 1)
    lead = 2 * channels - 1
    wanted = jnp.where(
        fold < channels,
        lead - fold,
        jnp.where(fold < REACH, REACH + lead - fold, REACH + channels - 1 - fold),
    )
    turn = (wanted == source).astype(jnp.float32).astype(jnp.bfloat16)

    def arrange(lanes):
        rows_ahead, rows_behind = neighbours(lanes)
        turned = jnp.dot(turn, rows_behind, preferred_element_type=jnp.float32).astype(jnp.bfloat16)
        partners_ref[:REACH, lanes] = rows_ahead[:REACH]
        partners_ref[REACH : 2 * REACH, lanes] = turned[:REACH]
        partners_ref[2 * REACH : 2 * REACH + channels, lanes] = rows_ahead[REACH:]
        partners_ref[2 * REACH + channels :, lanes] = turned[REACH:]

    row = lax.broadcasted_iota(jnp.int32, (channels, LANES), 0)
    lane = lax.broadcasted_iota(jnp.int32, (channels, LANES), 1)
    wrap_ahead = lane <= row
    wrap_behind = (lane >= channels) & (lane <= lead - row)
    flip = 7 - lax.broadcasted_iota(jnp.int32, (8, LANES), 0)
    part = lax.rem(lane // PACK, 2)

    def turned_rows(v):
        return jnp.take_along_axis(v, flip, axis=0)

    def skewed(ahead, behind, ends):
        a = jnp.where(wrap_ahead, ends, ahead)
        b = jnp.where(wrap_behind, ends, behind)
        aheads = []
        for r in range(0, channels, 8):
            v = pltpu.roll(turned_rows(a[r : r + 8]), (2 * LANES - r - 8) % LANES, 1, stride=1, stride_axis=0)
            aheads.append(turned_rows(v))
        b = pltpu.roll(b, LANES - 2 * channels, 1, stride=1, stride_axis=0)
        return jnp.concatenate(aheads, axis=0), b

    contract = (((1,), (1,)), ((), ()))

    def multiply(g):
        lanes = slice(g * LANES, (g + 1) * LANES)
        a = own_ref[:, lanes].astype(jnp.float32)
        rotated = jnp.where(part == 0, -pltpu.roll(a, LANES - PACK, 1), pltpu.roll(a, PACK, 1))
        zero = jnp.zeros_like(a)
        rows = []
        for f in range(PACK):
            mask = lax.rem(lane, PACK) == f
            rows += [jnp.where(mask, a, zero), jnp.where(mask, rotated, zero)]
        lhs = jnp.concatenate(rows, axis=0).astype(jnp.bfloat16)
        products[g % len(products)][:, : 2 * (REACH + channels)] = lax.dot_general(
            lhs, partners_ref[:, lanes], contract, preferred_element_type=jnp.float32
        )

    def copies(g):
        bins = pl.ds(g * PACK, PACK)
        return [
            pltpu.make_async_copy(held.at[:, bins], out.at[:, bins], sems.at[k, g])
            for k, (held, out) in enumerate(((ahead_ref, ahead_hbm), (behind_ref, behind_hbm)))
        ]

    def finish(g):
        product = products[g % len(products)]
        for f in range(PACK):
            for v in range(2):
                rows = pl.ds((2 * f + v) * channels, channels)
                ahead, behind = skewed(*(product[rows, pl.ds(t * LANES, LANES)] for t in range(3)))
                ahead_ref[v, g * PACK + f] = (ahead * div_ahead[...]).astype(jnp.bfloat16)
                behind_ref[v, g * PACK + f] = (behind * div_behind[...]).astype(jnp.bfloat16)
        for copy in copies(g):
            copy.start()

    flags = slice(packs * LANES, (packs + 1) * LANES)
    for at in range(0, packs * LANES, WIDE):
        arrange(slice(at, min(at + WIDE, packs * LANES)))
    arrange(flags)
    counts = lax.dot_general(
        own_ref[:, flags], partners_ref[:, flags], contract, preferred_element_type=jnp.float32
    )
    products[0][:channels, : 2 * (REACH + channels)] = counts
    ahead, behind = skewed(*(products[0][:channels, t * LANES : (t + 1) * LANES] for t in range(3)))
    div_ahead[...] = 1.0 / jnp.maximum(ahead, 1.0)
    div_behind[...] = 1.0 / jnp.maximum(behind, 1.0)

    for g in range(packs):
        if g == 0:
            multiply(0)
            multiply(1)
        if g + 2 < packs:
            multiply(g + 2)
        finish(g)
    for g in range(packs):
        for copy in copies(g):
            copy.wait()


def cross(values, bin_count, order):
    channels = values[0].shape[0]
    shape = jax.ShapeDtypeStruct((2, bin_count, channels, REACH), jnp.bfloat16)
    products = pltpu.VMEM((2 * PACK * channels, 3 * LANES), jnp.float32)
    held = pltpu.VMEM((2, bin_count, channels, REACH), jnp.bfloat16)
    return pl.pallas_call(
        functools.partial(cross_kernel, order),
        in_specs=[pl.BlockSpec(memory_space=pltpu.VMEM)] * len(values),
        out_specs=[pl.BlockSpec(memory_space=pl.ANY)] * 2,
        out_shape=[shape, shape],
        scratch_shapes=[
            pltpu.VMEM((2 * (REACH + channels), values[0].shape[1]), jnp.bfloat16),
            pltpu.VMEM((channels, REACH), jnp.float32),
            pltpu.VMEM((channels, REACH), jnp.float32),
            products,
            products,
            products,
            held,
            held,
            pltpu.SemaphoreType.DMA((2, bin_count // PACK)),
        ],
        compiler_params=pltpu.CompilerParams(vmem_limit_bytes=VMEM_BYTES),
        name="cross",
    )(*values)


def per_device(strain, channel_ok, window_ok):
    freq_devices = lax.axis_size("freq")
    own = whiten(strain, channel_ok, window_ok, freq_devices)
    mate = trade(own, beside)
    arrived = [trade(own, f) for f in (partner_pair, other_pair, partner_far, other_far)]
    shared = [trade(block, beside) for block in arrived]
    order = (3, 2, 0, 1)
    last = [arrived[k] for k in order] + [shared[k] for k in order]
    return cross([own, mate, *last], BINS // freq_devices, order)


def solution(mesh):
    return jax.shard_map(
        per_device,
        mesh=mesh,
        in_specs=(P("ch", None, None), P("ch"), P("ch", None)),
        out_specs=(P(None, "freq", "ch", None), P(None, "freq", "ch", None)),
        check_vma=False,
    )
```

```python
import functools
import math

import jax
import jax.numpy as jnp
import ml_dtypes
import numpy as np
from jax import lax
from jax.experimental import pallas as pl
from jax.experimental.pallas import tpu as pltpu
from jax.sharding import PartitionSpec as P

WINDOWS = 8
BINS = 256
REACH = 128
TIME_HALF = 128
BIN_HALF = 32
LANES = 128
PACK = LANES // (2 * WINDOWS)
HALVES = 1
CHUNK = 2048
WIDE = 512
VMEM_BYTES = 40 * 1024 * 1024


def bin_columns(bin_count):
    halo = np.concatenate([np.arange(-BIN_HALF, 0), np.arange(bin_count, bin_count + BIN_HALF)])
    own = np.arange(bin_count).reshape(-1, 1, PACK)
    parts = np.arange(2).reshape(1, 2, 1)
    shape = (bin_count // PACK, 2, PACK)
    bins = np.concatenate([halo, halo, np.broadcast_to(own, shape).ravel()])
    part = np.concatenate(
        [np.zeros_like(halo), np.ones_like(halo), np.broadcast_to(parts, shape).ravel()]
    )
    return bins, part


def dft_tables(freq_devices, samples):
    bin_count = BINS // freq_devices
    bins, part = bin_columns(bin_count)
    sample_ids = np.arange(samples)
    tables = []
    for device in range(freq_devices):
        freq = device * bin_count + bins + 1
        inside = (freq >= 1) & (freq <= BINS)
        turn = (freq[None, :] * sample_ids[:, None]) % samples
        phase = turn.astype(np.float32) * np.float32(2.0 * math.pi / samples)
        wave = np.where(part[None, :] == 0, np.cos(phase), -np.sin(phase)).astype(np.float32)
        wave = wave * np.float32(1.0 / math.sqrt(samples)) * inside[None, :]
        tables.append(wave.astype(ml_dtypes.bfloat16))
    return np.stack(tables)


def smoother(bin_count):
    bins, _ = bin_columns(bin_count)
    own = bins[4 * BIN_HALF :]
    return (np.abs(bins[:, None] - own[None, :]) <= BIN_HALF).astype(ml_dtypes.bfloat16)


def whiten_kernel(
    x_hbm, ok_hbm, win_hbm, table_hbm, smooth_hbm, out_ref,
    x_ref, ok_ref, win_ref, table_ref, smooth_ref, mag_ref, level_ref, spec_ref, x_sems, table_sems, sems,
):
    channels, windows, samples = x_ref.shape
    rows = channels * windows
    halo = 4 * BIN_HALF
    own = table_ref.shape[1] - halo
    tile = 2 * TIME_HALF
    count = 2 * TIME_HALF + 1
    tiles = samples // tile
    q = lax.axis_index("freq")

    def chunk(k):
        return pl.ds(k * CHUNK, CHUNK)

    x_copies = [
        pltpu.make_async_copy(x_hbm.at[:, :, chunk(k)], x_ref.at[:, :, chunk(k)], x_sems.at[k])
        for k in range(samples // CHUNK)
    ]
    table_copies = [
        pltpu.make_async_copy(table_hbm.at[q, chunk(k)], table_ref.at[chunk(k)], table_sems.at[k])
        for k in range(samples // CHUNK)
    ]
    small_copies = [
        pltpu.make_async_copy(source, target, sems.at[k])
        for k, (source, target) in enumerate(
            ((ok_hbm, ok_ref), (win_hbm, win_ref), (smooth_hbm, smooth_ref))
        )
    ]
    for copy in x_copies + table_copies + small_copies:
        copy.start()

    mag_ref[:, :TIME_HALF] = jnp.zeros((rows, TIME_HALF), jnp.bfloat16)
    mag_ref[:, TIME_HALF + samples :] = jnp.zeros((rows, TIME_HALF), jnp.bfloat16)
    source = lax.broadcasted_iota(jnp.int32, (2 * tile, tile), 0) - TIME_HALF
    target = lax.broadcasted_iota(jnp.int32, (2 * tile, tile), 1)
    band = (jnp.abs(source - target) <= TIME_HALF).astype(jnp.float32).astype(jnp.bfloat16)

    def loaded(t):
        return x_ref[:, :, t * tile : (t + 1) * tile].astype(jnp.float32).reshape(rows, tile)

    for t in range(tiles):
        if t * tile % CHUNK == 0:
            x_copies[t * tile // CHUNK].wait()
        mag_ref[:, TIME_HALF + t * tile : TIME_HALF + (t + 1) * tile] = jnp.abs(loaded(t)).astype(
            jnp.bfloat16
        )
    for t in range(tiles):
        sums = jnp.dot(
            mag_ref[:, t * tile : (t + 2) * tile], band, preferred_element_type=jnp.float32
        )
        level_ref[:, t * tile : (t + 1) * tile] = (
            loaded(t) * (count / (sums + count * 1e-06))
        ).astype(jnp.bfloat16)
    for copy in table_copies + small_copies:
        copy.wait()
    flags = (ok_ref[...] * win_ref[...]).astype(jnp.float32).astype(jnp.bfloat16)
    lane = lax.broadcasted_iota(jnp.int32, (windows, LANES), 1)
    window = lax.broadcasted_iota(jnp.int32, (windows, LANES), 0)
    contract = (((0,), (0,)), ((), ()))
    picked = (lane == window).astype(jnp.float32).astype(jnp.bfloat16)
    out_ref[:, windows * own :] = lax.dot_general(
        flags, picked, contract, preferred_element_type=jnp.float32
    ).astype(jnp.bfloat16)
    width = 2 * PACK
    usable = []
    for g in range(LANES // width):
        spread = (lax.rem(lane // width + windows - g, windows) == window).astype(jnp.float32)
        usable.append(
            lax.dot_general(
                flags, spread.astype(jnp.bfloat16), contract, preferred_element_type=jnp.float32
            )
        )

    ones = smooth_ref[...]
    half = channels // HALVES
    block = lax.broadcasted_iota(jnp.int32, (half, LANES), 1) // width
    for h in range(HALVES):
        part = slice(h * half * windows, (h + 1) * half * windows)
        spectra = jnp.dot(level_ref[part], table_ref[...], preferred_element_type=jnp.float32)
        power = spectra * spectra
        high = power.astype(jnp.bfloat16)
        low = (power - high.astype(jnp.float32)).astype(jnp.bfloat16)
        smooth = jnp.dot(high, ones, preferred_element_type=jnp.float32) + jnp.dot(
            low, ones, preferred_element_type=jnp.float32
        )
        white = spectra[:, halo:] * lax.rsqrt(smooth * (1.0 / (2 * BIN_HALF + 1)) + 1e-06)
        for t in range(0, own, LANES):
            tile_width = min(LANES, own - t)
            tile_white = white[:, t : t + tile_width]
            if tile_width < LANES:
                rest = jnp.zeros((half * windows, LANES - tile_width), jnp.float32)
                tile_white = jnp.concatenate([tile_white, rest], axis=1)
            turned = pltpu.roll(tile_white, 0, 1, stride=width, stride_axis=0)
            spec_ref[h, t // LANES] = turned
            windows_of = [spec_ref[h, t // LANES, pl.ds(w, half, stride=windows), :] for w in range(windows)]
            for g in range(tile_width // width):
                packed = windows_of[0]
                for w in range(1, windows):
                    packed = jnp.where(block == (g + w) % windows, windows_of[w], packed)
                packed = packed * usable[g][h * half : (h + 1) * half]
                at = (t // width + g) * LANES
                out_ref[h * half : (h + 1) * half, at : at + LANES] = packed.astype(jnp.bfloat16)


def whiten(strain, channel_ok, window_ok, freq_devices):
    channels, windows, samples = strain.shape
    bin_count = BINS // freq_devices
    tables = jnp.asarray(dft_tables(freq_devices, samples))
    ones = jnp.asarray(smoother(bin_count))
    columns = tables.shape[2]
    own = 2 * bin_count
    rows = channels * windows
    chunks = samples // CHUNK
    return pl.pallas_call(
        whiten_kernel,
        in_specs=[pl.BlockSpec(memory_space=pltpu.HBM)] * 5,
        out_specs=pl.BlockSpec(memory_space=pltpu.VMEM),
        out_shape=pltpu.VMEM((channels, windows * own + LANES), jnp.bfloat16),
        scratch_shapes=[
            pltpu.VMEM((channels, windows, samples), jnp.bfloat16),
            pltpu.VMEM((1, channels), jnp.int32),
            pltpu.VMEM((windows, channels), jnp.int32),
            pltpu.VMEM((samples, columns), jnp.bfloat16),
            pltpu.VMEM((columns, own), jnp.bfloat16),
            pltpu.VMEM((rows, samples + 2 * TIME_HALF), jnp.bfloat16),
            pltpu.VMEM((rows, samples), jnp.bfloat16),
            pltpu.VMEM((HALVES, -(-own // LANES), rows // HALVES, LANES), jnp.float32),
            pltpu.SemaphoreType.DMA((chunks,)),
            pltpu.SemaphoreType.DMA((chunks,)),
            pltpu.SemaphoreType.DMA((3,)),
        ],
        compiler_params=pltpu.CompilerParams(vmem_limit_bytes=VMEM_BYTES),
        name="whiten",
    )(
        *(
            pltpu.with_memory_space_constraint(value, pltpu.HBM)
            for value in (strain, channel_ok.reshape(1, channels), window_ok.T, tables, ones)
        )
    )


def trade(value, partner):
    count = lax.axis_size("ch")
    inside = lambda i: 0 <= partner(i) < count
    return lax.ppermute(value, "ch", [(i, partner(i) if inside(i) else beside(i)) for i in range(count)])


def beside(i):
    return i + 1 - 2 * (i % 2)


def partner_pair(i):
    return i + 2 - 4 * (i // 2 % 2)


def other_pair(i):
    return i - 2 + 4 * (i // 2 % 2)


def partner_far(i):
    return i + 4 - 8 * (i // 4 % 2)


def other_far(i):
    return i - 4 + 8 * (i // 4 % 2)


TRADES = (partner_pair, other_pair, partner_far, other_far)


def cross_kernel(order, own_ref, mate_ref, *refs):
    arrived = [refs[at + order.index(k)] for at in (0, 4) for k in range(4)]
    (ahead_hbm, behind_hbm, partners_ref, div_ahead, div_behind, count_ref, *products) = refs[8:-3]
    ahead_ref, behind_ref, sems = refs[-3:]
    channels = own_ref.shape[0]
    packs = own_ref.shape[1] // LANES - 1
    index = lax.axis_index("ch")
    first = lax.rem(index, 2) == 0
    pair = index // 2
    near_up = lax.rem(pair, 2) == 0
    far_up = lax.rem(pair // 2, 2) == 0
    count = lax.axis_size("ch")
    met_index = [partner(index) for partner in TRADES]
    inside = [(i >= 0) & (i < count) for i in met_index]

    def neighbours(lanes):
        pick = lambda a, b: jnp.where(first, a, b)
        own, mate = own_ref[:, lanes], mate_ref[:, lanes]
        mine, theirs = [r[:, lanes] for r in arrived[:4]], [r[:, lanes] for r in arrived[4:]]
        met = [(pick(a, b), pick(b, a)) for a, b in zip(mine, theirs, strict=True)]
        met = [tuple(jnp.where(ok, x, jnp.zeros_like(x)) for x in blocks) for ok, blocks in zip(inside, met, strict=True)]
        choose = lambda up, a, b: tuple(jnp.where(up, x, y) for x, y in zip(a, b, strict=True))
        up1, down1 = choose(near_up, met[0], met[1]), choose(near_up, met[1], met[0])
        up2, down2 = choose(far_up, met[2], met[3]), choose(far_up, met[3], met[2])
        ahead = [own, pick(mate, up1[0]), pick(up1[0], up1[1]), pick(up1[1], up2[0]), pick(up2[0], up2[1])]
        behind = [pick(down2[0], down2[1]), pick(down2[1], down1[0]), pick(down1[0], down1[1]), pick(down1[1], mate), own]
        return jnp.concatenate(ahead, axis=0), jnp.concatenate(behind, axis=0)

    total = REACH + channels
    fold = lax.broadcasted_iota(jnp.int32, (total, total), 0)
    source = lax.broadcasted_iota(jnp.int32, (total, total), 1)
    lead = 2 * channels - 1
    wanted = jnp.where(
        fold < channels,
        lead - fold,
        jnp.where(fold < REACH, REACH + lead - fold, REACH + channels - 1 - fold),
    )
    turn = (wanted == source).astype(jnp.float32).astype(jnp.bfloat16)

    def arrange(lanes):
        rows_ahead, rows_behind = neighbours(lanes)
        turned = jnp.dot(turn, rows_behind, preferred_element_type=jnp.float32).astype(jnp.bfloat16)
        partners_ref[:REACH, lanes] = rows_ahead[:REACH]
        partners_ref[REACH : 2 * REACH, lanes] = turned[:REACH]
        partners_ref[2 * REACH : 2 * REACH + channels, lanes] = rows_ahead[REACH:]
        partners_ref[2 * REACH + channels :, lanes] = turned[REACH:]

    row = lax.broadcasted_iota(jnp.int32, (channels, LANES), 0)
    lane = lax.broadcasted_iota(jnp.int32, (channels, LANES), 1)
    wrap_ahead = lane <= row
    wrap_behind = (lane >= channels) & (lane <= lead - row)
    flip = 7 - lax.broadcasted_iota(jnp.int32, (8, LANES), 0)
    part = lax.rem(lane // PACK, 2)

    def turned_rows(v):
        return jnp.take_along_axis(v, flip, axis=0)

    def skewed(ahead, behind, ends):
        a = jnp.where(wrap_ahead, ends, ahead)
        b = jnp.where(wrap_behind, ends, behind)
        aheads = []
        for r in range(0, channels, 8):
            v = pltpu.roll(turned_rows(a[r : r + 8]), (2 * LANES - r - 8) % LANES, 1, stride=1, stride_axis=0)
            aheads.append(turned_rows(v))
        b = pltpu.roll(b, LANES - 2 * channels, 1, stride=1, stride_axis=0)
        return jnp.concatenate(aheads, axis=0), b

    contract = (((1,), (1,)), ((), ()))

    def multiply(g):
        lanes = slice(g * LANES, (g + 1) * LANES)
        a = own_ref[:, lanes].astype(jnp.float32)
        rotated = jnp.where(part == 0, -pltpu.roll(a, LANES - PACK, 1), pltpu.roll(a, PACK, 1))
        zero = jnp.zeros_like(a)
        rows = []
        for f in range(PACK):
            mask = lax.rem(lane, PACK) == f
            rows += [jnp.where(mask, a, zero), jnp.where(mask, rotated, zero)]
        lhs = jnp.concatenate(rows, axis=0).astype(jnp.bfloat16)
        products[g % len(products)][:, : 2 * (REACH + channels)] = lax.dot_general(
            lhs, partners_ref[:, lanes], contract, preferred_element_type=jnp.float32
        )

    def copies(g):
        bins = pl.ds(g * PACK, PACK)
        return [
            pltpu.make_async_copy(held.at[:, bins], out.at[:, bins], sems.at[k, g])
            for k, (held, out) in enumerate(((ahead_ref, ahead_hbm), (behind_ref, behind_hbm)))
        ]

    def finish(g):
        product = products[g % len(products)]
        for f in range(PACK):
            for v in range(2):
                rows = pl.ds((2 * f + v) * channels, channels)
                ahead, behind = skewed(*(product[rows, pl.ds(t * LANES, LANES)] for t in range(3)))
                ahead_ref[v, g * PACK + f] = (ahead * div_ahead[...]).astype(jnp.bfloat16)
                behind_ref[v, g * PACK + f] = (behind * div_behind[...]).astype(jnp.bfloat16)
        for copy in copies(g):
            copy.start()

    flags = slice(packs * LANES, (packs + 1) * LANES)
    lead_packs = WIDE // LANES
    for g in range(packs):
        if g == 0:
            arrange(flags)
            count_ref[:, : 2 * (REACH + channels)] = lax.dot_general(
                own_ref[:, flags], partners_ref[:, flags], contract, preferred_element_type=jnp.float32
            )
            arrange(slice(0, WIDE))
            multiply(0)
            multiply(1)
            ahead, behind = skewed(*(count_ref[:, t * LANES : (t + 1) * LANES] for t in range(3)))
            div_ahead[...] = 1.0 / jnp.maximum(ahead, 1.0)
            div_behind[...] = 1.0 / jnp.maximum(behind, 1.0)
        at = g + lead_packs
        if at < packs and at % lead_packs == 0:
            arrange(slice(at * LANES, (at + lead_packs) * LANES))
        if g + 2 < packs:
            multiply(g + 2)
        finish(g)
    for g in range(packs):
        for copy in copies(g):
            copy.wait()


def cross(values, bin_count, order):
    channels = values[0].shape[0]
    shape = jax.ShapeDtypeStruct((2, bin_count, channels, REACH), jnp.bfloat16)
    products = pltpu.VMEM((2 * PACK * channels, 3 * LANES), jnp.float32)
    held = pltpu.VMEM((2, bin_count, channels, REACH), jnp.bfloat16)
    return pl.pallas_call(
        functools.partial(cross_kernel, order),
        in_specs=[pl.BlockSpec(memory_space=pltpu.VMEM)] * len(values),
        out_specs=[pl.BlockSpec(memory_space=pl.ANY)] * 2,
        out_shape=[shape, shape],
        scratch_shapes=[
            pltpu.VMEM((2 * (REACH + channels), values[0].shape[1]), jnp.bfloat16),
            pltpu.VMEM((channels, REACH), jnp.float32),
            pltpu.VMEM((channels, REACH), jnp.float32),
            pltpu.VMEM((channels, 3 * LANES), jnp.float32),
            products,
            products,
            products,
            held,
            held,
            pltpu.SemaphoreType.DMA((2, bin_count // PACK)),
        ],
        compiler_params=pltpu.CompilerParams(vmem_limit_bytes=VMEM_BYTES),
        name="cross",
    )(*values)


def per_device(strain, channel_ok, window_ok):
    freq_devices = lax.axis_size("freq")
    own = whiten(strain, channel_ok, window_ok, freq_devices)
    mate = trade(own, beside)
    arrived = [trade(own, partner) for partner in TRADES]
    shared = [trade(block, beside) for block in arrived]
    order = (2, 3, 0, 1)
    last = [arrived[k] for k in order] + [shared[k] for k in order]
    return cross([own, mate, *last], BINS // freq_devices, order)


def solution(mesh):
    return jax.shard_map(
        per_device,
        mesh=mesh,
        in_specs=(P("ch", None, None), P("ch"), P("ch", None)),
        out_specs=(P(None, "freq", "ch", None), P(None, "freq", "ch", None)),
        check_vma=False,
    )
```

```python
import functools
import math

import jax
import jax.numpy as jnp
import ml_dtypes
import numpy as np
from jax import lax
from jax.experimental import pallas as pl
from jax.experimental.pallas import tpu as pltpu
from jax.sharding import PartitionSpec as P

WINDOWS = 8
BINS = 256
REACH = 128
TIME_HALF = 128
BIN_HALF = 32
LANES = 128
PACK = LANES // (2 * WINDOWS)
HALVES = 1
CHUNK = 2048
WIDE = 512
VMEM_BYTES = 40 * 1024 * 1024


def bin_columns(bin_count):
    halo = np.concatenate([np.arange(-BIN_HALF, 0), np.arange(bin_count, bin_count + BIN_HALF)])
    own = np.arange(bin_count).reshape(-1, 1, PACK)
    parts = np.arange(2).reshape(1, 2, 1)
    shape = (bin_count // PACK, 2, PACK)
    bins = np.concatenate([halo, halo, np.broadcast_to(own, shape).ravel()])
    part = np.concatenate(
        [np.zeros_like(halo), np.ones_like(halo), np.broadcast_to(parts, shape).ravel()]
    )
    return bins, part


def dft_tables(freq_devices, samples):
    bin_count = BINS // freq_devices
    bins, part = bin_columns(bin_count)
    sample_ids = np.arange(samples)
    tables = []
    for device in range(freq_devices):
        freq = device * bin_count + bins + 1
        inside = (freq >= 1) & (freq <= BINS)
        turn = (freq[None, :] * sample_ids[:, None]) % samples
        phase = turn.astype(np.float32) * np.float32(2.0 * math.pi / samples)
        wave = np.where(part[None, :] == 0, np.cos(phase), -np.sin(phase)).astype(np.float32)
        wave = wave * np.float32(1.0 / math.sqrt(samples)) * inside[None, :]
        tables.append(wave.astype(ml_dtypes.bfloat16))
    return np.stack(tables)


def smoother(bin_count):
    bins, _ = bin_columns(bin_count)
    own = bins[4 * BIN_HALF :]
    return (np.abs(bins[:, None] - own[None, :]) <= BIN_HALF).astype(ml_dtypes.bfloat16)


def whiten_kernel(
    x_hbm, ok_hbm, win_hbm, table_hbm, smooth_hbm, out_ref,
    x_ref, ok_ref, win_ref, table_ref, smooth_ref, mag_ref, level_ref, spec_ref, x_sems, table_sems, sems,
):
    channels, windows, samples = x_ref.shape
    rows = channels * windows
    halo = 4 * BIN_HALF
    own = table_ref.shape[1] - halo
    tile = 2 * TIME_HALF
    count = 2 * TIME_HALF + 1
    tiles = samples // tile
    q = lax.axis_index("freq")

    def chunk(k):
        return pl.ds(k * CHUNK, CHUNK)

    x_copies = [
        pltpu.make_async_copy(x_hbm.at[:, :, chunk(k)], x_ref.at[:, :, chunk(k)], x_sems.at[k])
        for k in range(samples // CHUNK)
    ]
    table_copies = [
        pltpu.make_async_copy(table_hbm.at[q, chunk(k)], table_ref.at[chunk(k)], table_sems.at[k])
        for k in range(samples // CHUNK)
    ]
    small_copies = [
        pltpu.make_async_copy(source, target, sems.at[k])
        for k, (source, target) in enumerate(
            ((ok_hbm, ok_ref), (win_hbm, win_ref), (smooth_hbm, smooth_ref))
        )
    ]
    for copy in x_copies + table_copies + small_copies:
        copy.start()

    mag_ref[:, :TIME_HALF] = jnp.zeros((rows, TIME_HALF), jnp.bfloat16)
    mag_ref[:, TIME_HALF + samples :] = jnp.zeros((rows, TIME_HALF), jnp.bfloat16)
    source = lax.broadcasted_iota(jnp.int32, (2 * tile, tile), 0) - TIME_HALF
    target = lax.broadcasted_iota(jnp.int32, (2 * tile, tile), 1)
    band = (jnp.abs(source - target) <= TIME_HALF).astype(jnp.float32).astype(jnp.bfloat16)

    def loaded(t):
        return x_ref[:, :, t * tile : (t + 1) * tile].astype(jnp.float32).reshape(rows, tile)

    for t in range(tiles):
        if t * tile % CHUNK == 0:
            x_copies[t * tile // CHUNK].wait()
        mag_ref[:, TIME_HALF + t * tile : TIME_HALF + (t + 1) * tile] = jnp.abs(loaded(t)).astype(
            jnp.bfloat16
        )
    for t in range(tiles):
        sums = jnp.dot(
            mag_ref[:, t * tile : (t + 2) * tile], band, preferred_element_type=jnp.float32
        )
        level_ref[:, t * tile : (t + 1) * tile] = (
            loaded(t) * (count / (sums + count * 1e-06))
        ).astype(jnp.bfloat16)
    for copy in table_copies + small_copies:
        copy.wait()
    flags = (ok_ref[...] * win_ref[...]).astype(jnp.float32).astype(jnp.bfloat16)
    lane = lax.broadcasted_iota(jnp.int32, (windows, LANES), 1)
    window = lax.broadcasted_iota(jnp.int32, (windows, LANES), 0)
    contract = (((0,), (0,)), ((), ()))
    picked = (lane == window).astype(jnp.float32).astype(jnp.bfloat16)
    out_ref[:, windows * own :] = lax.dot_general(
        flags, picked, contract, preferred_element_type=jnp.float32
    ).astype(jnp.bfloat16)
    width = 2 * PACK
    usable = []
    for g in range(LANES // width):
        spread = (lax.rem(lane // width + windows - g, windows) == window).astype(jnp.float32)
        usable.append(
            lax.dot_general(
                flags, spread.astype(jnp.bfloat16), contract, preferred_element_type=jnp.float32
            )
        )

    ones = smooth_ref[...]
    half = channels // HALVES
    block = lax.broadcasted_iota(jnp.int32, (half, LANES), 1) // width
    for h in range(HALVES):
        part = slice(h * half * windows, (h + 1) * half * windows)
        spectra = jnp.dot(level_ref[part], table_ref[...], preferred_element_type=jnp.float32)
        power = spectra * spectra
        high = power.astype(jnp.bfloat16)
        low = (power - high.astype(jnp.float32)).astype(jnp.bfloat16)
        smooth = jnp.dot(high, ones, preferred_element_type=jnp.float32) + jnp.dot(
            low, ones, preferred_element_type=jnp.float32
        )
        white = spectra[:, halo:] * lax.rsqrt(smooth * (1.0 / (2 * BIN_HALF + 1)) + 1e-06)
        for t in range(0, own, LANES):
            tile_width = min(LANES, own - t)
            tile_white = white[:, t : t + tile_width]
            if tile_width < LANES:
                rest = jnp.zeros((half * windows, LANES - tile_width), jnp.float32)
                tile_white = jnp.concatenate([tile_white, rest], axis=1)
            turned = pltpu.roll(tile_white, 0, 1, stride=width, stride_axis=0)
            spec_ref[h, t // LANES] = turned
            windows_of = [spec_ref[h, t // LANES, pl.ds(w, half, stride=windows), :] for w in range(windows)]
            for g in range(tile_width // width):
                packed = windows_of[0]
                for w in range(1, windows):
                    packed = jnp.where(block == (g + w) % windows, windows_of[w], packed)
                packed = packed * usable[g][h * half : (h + 1) * half]
                at = (t // width + g) * LANES
                out_ref[h * half : (h + 1) * half, at : at + LANES] = packed.astype(jnp.bfloat16)


def whiten(strain, channel_ok, window_ok, freq_devices):
    channels, windows, samples = strain.shape
    bin_count = BINS // freq_devices
    tables = jnp.asarray(dft_tables(freq_devices, samples))
    ones = jnp.asarray(smoother(bin_count))
    columns = tables.shape[2]
    own = 2 * bin_count
    rows = channels * windows
    chunks = samples // CHUNK
    return pl.pallas_call(
        whiten_kernel,
        in_specs=[pl.BlockSpec(memory_space=pltpu.HBM)] * 5,
        out_specs=pl.BlockSpec(memory_space=pltpu.VMEM),
        out_shape=pltpu.VMEM((channels, windows * own + LANES), jnp.bfloat16),
        scratch_shapes=[
            pltpu.VMEM((channels, windows, samples), jnp.bfloat16),
            pltpu.VMEM((1, channels), jnp.int32),
            pltpu.VMEM((windows, channels), jnp.int32),
            pltpu.VMEM((samples, columns), jnp.bfloat16),
            pltpu.VMEM((columns, own), jnp.bfloat16),
            pltpu.VMEM((rows, samples + 2 * TIME_HALF), jnp.bfloat16),
            pltpu.VMEM((rows, samples), jnp.bfloat16),
            pltpu.VMEM((HALVES, -(-own // LANES), rows // HALVES, LANES), jnp.float32),
            pltpu.SemaphoreType.DMA((chunks,)),
            pltpu.SemaphoreType.DMA((chunks,)),
            pltpu.SemaphoreType.DMA((3,)),
        ],
        compiler_params=pltpu.CompilerParams(vmem_limit_bytes=VMEM_BYTES),
        name="whiten",
    )(
        *(
            pltpu.with_memory_space_constraint(value, pltpu.HBM)
            for value in (strain, channel_ok.reshape(1, channels), window_ok.T, tables, ones)
        )
    )


def trade(value, partner):
    count = lax.axis_size("ch")
    inside = lambda i: 0 <= partner(i) < count
    return lax.ppermute(value, "ch", [(i, partner(i) if inside(i) else beside(i)) for i in range(count)])


def beside(i):
    return i + 1 - 2 * (i % 2)


def partner_pair(i):
    return i + 2 - 4 * (i // 2 % 2)


def other_pair(i):
    return i - 2 + 4 * (i // 2 % 2)


def partner_far(i):
    return i + 4 - 8 * (i // 4 % 2)


def other_far(i):
    return i - 4 + 8 * (i // 4 % 2)


SHARE = (2, 0, 1)
TRADES = (partner_pair, other_pair, partner_far, other_far)


def cross_kernel(order, own_ref, mate_ref, *refs):
    arrived, shared = [refs[order.index(k)] for k in range(4)], [refs[4 + SHARE.index(k)] for k in range(3)]
    (ahead_hbm, behind_hbm, partners_ref, div_ahead, div_behind, count_ref, *products) = refs[7:-3]
    ahead_ref, behind_ref, sems = refs[-3:]
    channels = own_ref.shape[0]
    packs = own_ref.shape[1] // LANES - 1
    index = lax.axis_index("ch")
    first = lax.rem(index, 2) == 0
    pair = index // 2
    near_up = lax.rem(pair, 2) == 0
    far_up = lax.rem(pair // 2, 2) == 0
    count = lax.axis_size("ch")
    met_index = [partner(index) for partner in TRADES]
    inside = [(i >= 0) & (i < count) for i in met_index]

    def neighbours(lanes):
        pick = lambda a, b: jnp.where(first, a, b)
        own, mate = own_ref[:, lanes], mate_ref[:, lanes]
        mine, theirs = [r[:, lanes] for r in arrived], [r[:, lanes] for r in shared]
        theirs.append(theirs[2])
        met = [(pick(a, b), pick(b, a)) for a, b in zip(mine, theirs, strict=True)]
        met = [tuple(jnp.where(ok, x, jnp.zeros_like(x)) for x in blocks) for ok, blocks in zip(inside, met, strict=True)]
        choose = lambda up, a, b: tuple(jnp.where(up, x, y) for x, y in zip(a, b, strict=True))
        up1, down1 = choose(near_up, met[0], met[1]), choose(near_up, met[1], met[0])
        up2, down2 = choose(far_up, met[2], met[3]), choose(far_up, met[3], met[2])
        ahead = [own, pick(mate, up1[0]), pick(up1[0], up1[1]), pick(up1[1], up2[0]), pick(up2[0], up2[1])]
        behind = [pick(down2[0], down2[1]), pick(down2[1], down1[0]), pick(down1[0], down1[1]), pick(down1[1], mate), own]
        return jnp.concatenate(ahead, axis=0), jnp.concatenate(behind, axis=0)

    total = REACH + channels
    fold = lax.broadcasted_iota(jnp.int32, (total, total), 0)
    source = lax.broadcasted_iota(jnp.int32, (total, total), 1)
    lead = 2 * channels - 1
    wanted = jnp.where(
        fold < channels,
        lead - fold,
        jnp.where(fold < REACH, REACH + lead - fold, REACH + channels - 1 - fold),
    )
    turn = (wanted == source).astype(jnp.float32).astype(jnp.bfloat16)

    def arrange(lanes):
        rows_ahead, rows_behind = neighbours(lanes)
        turned = jnp.dot(turn, rows_behind, preferred_element_type=jnp.float32).astype(jnp.bfloat16)
        partners_ref[:REACH, lanes] = rows_ahead[:REACH]
        partners_ref[REACH : 2 * REACH, lanes] = turned[:REACH]
        partners_ref[2 * REACH : 2 * REACH + channels, lanes] = rows_ahead[REACH:]
        partners_ref[2 * REACH + channels :, lanes] = turned[REACH:]

    row = lax.broadcasted_iota(jnp.int32, (channels, LANES), 0)
    lane = lax.broadcasted_iota(jnp.int32, (channels, LANES), 1)
    wrap_ahead = lane <= row
    wrap_behind = (lane >= channels) & (lane <= lead - row)
    flip = 7 - lax.broadcasted_iota(jnp.int32, (8, LANES), 0)
    part = lax.rem(lane // PACK, 2)

    def turned_rows(v):
        return jnp.take_along_axis(v, flip, axis=0)

    def skewed(ahead, behind, ends):
        a = jnp.where(wrap_ahead, ends, ahead)
        b = jnp.where(wrap_behind, ends, behind)
        aheads = []
        for r in range(0, channels, 8):
            v = pltpu.roll(turned_rows(a[r : r + 8]), (2 * LANES - r - 8) % LANES, 1, stride=1, stride_axis=0)
            aheads.append(turned_rows(v))
        b = pltpu.roll(b, LANES - 2 * channels, 1, stride=1, stride_axis=0)
        return jnp.concatenate(aheads, axis=0), b

    contract = (((1,), (1,)), ((), ()))

    def multiply(g):
        lanes = slice(g * LANES, (g + 1) * LANES)
        a = own_ref[:, lanes].astype(jnp.float32)
        rotated = jnp.where(part == 0, -pltpu.roll(a, LANES - PACK, 1), pltpu.roll(a, PACK, 1))
        zero = jnp.zeros_like(a)
        rows = []
        for f in range(PACK):
            mask = lax.rem(lane, PACK) == f
            rows += [jnp.where(mask, a, zero), jnp.where(mask, rotated, zero)]
        lhs = jnp.concatenate(rows, axis=0).astype(jnp.bfloat16)
        products[g % len(products)][:, : 2 * (REACH + channels)] = lax.dot_general(
            lhs, partners_ref[:, lanes], contract, preferred_element_type=jnp.float32
        )

    def copies(g):
        bins = pl.ds(g * PACK, PACK)
        return [
            pltpu.make_async_copy(held.at[:, bins], out.at[:, bins], sems.at[k, g])
            for k, (held, out) in enumerate(((ahead_ref, ahead_hbm), (behind_ref, behind_hbm)))
        ]

    def finish(g):
        product = products[g % len(products)]
        for f in range(PACK):
            for v in range(2):
                rows = pl.ds((2 * f + v) * channels, channels)
                ahead, behind = skewed(*(product[rows, pl.ds(t * LANES, LANES)] for t in range(3)))
                ahead_ref[v, g * PACK + f] = (ahead * div_ahead[...]).astype(jnp.bfloat16)
                behind_ref[v, g * PACK + f] = (behind * div_behind[...]).astype(jnp.bfloat16)
        for copy in copies(g):
            copy.start()

    flags = slice(packs * LANES, (packs + 1) * LANES)
    lead_packs = WIDE // LANES
    for g in range(packs):
        if g == 0:
            arrange(flags)
            count_ref[:, : 2 * (REACH + channels)] = lax.dot_general(
                own_ref[:, flags], partners_ref[:, flags], contract, preferred_element_type=jnp.float32
            )
            arrange(slice(0, WIDE))
            multiply(0)
            multiply(1)
            ahead, behind = skewed(*(count_ref[:, t * LANES : (t + 1) * LANES] for t in range(3)))
            div_ahead[...] = 1.0 / jnp.maximum(ahead, 1.0)
            div_behind[...] = 1.0 / jnp.maximum(behind, 1.0)
        at = g + lead_packs
        if at < packs and at % lead_packs == 0:
            arrange(slice(at * LANES, (at + lead_packs) * LANES))
        if g + 2 < packs:
            multiply(g + 2)
        finish(g)
    for g in range(packs):
        for copy in copies(g):
            copy.wait()


def cross(values, bin_count, order):
    channels = values[0].shape[0]
    shape = jax.ShapeDtypeStruct((2, bin_count, channels, REACH), jnp.bfloat16)
    products = pltpu.VMEM((2 * PACK * channels, 3 * LANES), jnp.float32)
    held = pltpu.VMEM((2, bin_count, channels, REACH), jnp.bfloat16)
    return pl.pallas_call(
        functools.partial(cross_kernel, order),
        in_specs=[pl.BlockSpec(memory_space=pltpu.VMEM)] * len(values),
        out_specs=[pl.BlockSpec(memory_space=pl.ANY)] * 2,
        out_shape=[shape, shape],
        scratch_shapes=[
            pltpu.VMEM((2 * (REACH + channels), values[0].shape[1]), jnp.bfloat16),
            pltpu.VMEM((channels, REACH), jnp.float32),
            pltpu.VMEM((channels, REACH), jnp.float32),
            pltpu.VMEM((channels, 3 * LANES), jnp.float32),
            products,
            products,
            products,
            held,
            held,
            pltpu.SemaphoreType.DMA((2, bin_count // PACK)),
        ],
        compiler_params=pltpu.CompilerParams(vmem_limit_bytes=VMEM_BYTES),
        name="cross",
    )(*values)


def per_device(strain, channel_ok, window_ok):
    freq_devices = lax.axis_size("freq")
    own = whiten(strain, channel_ok, window_ok, freq_devices)
    mate = trade(own, beside)
    arrived = [trade(own, partner) for partner in TRADES]
    index = lax.axis_index("ch")
    ahead_first = (index // 4 + index) % 2 == 0
    shared = [trade(block, beside) for block in (*arrived[:2], jnp.where(ahead_first, arrived[2], arrived[3]))]
    order = (3, 0, 2, 1)
    last = [arrived[k] for k in order] + [shared[k] for k in SHARE]
    return cross([own, mate, *last], BINS // freq_devices, order)


def solution(mesh):
    return jax.shard_map(
        per_device,
        mesh=mesh,
        in_specs=(P("ch", None, None), P("ch"), P("ch", None)),
        out_specs=(P(None, "freq", "ch", None), P(None, "freq", "ch", None)),
        check_vma=False,
    )
```

```python
import functools
import math

import jax
import jax.numpy as jnp
import ml_dtypes
import numpy as np
from jax import lax
from jax.experimental import pallas as pl
from jax.experimental.pallas import tpu as pltpu
from jax.sharding import PartitionSpec as P

WINDOWS = 8
BINS = 256
REACH = 128
TIME_HALF = 128
BIN_HALF = 32
LANES = 128
PACK = LANES // (2 * WINDOWS)
HALVES = 1
CHUNK = 2048
WIDE = 512
VMEM_BYTES = 40 * 1024 * 1024


def bin_columns(bin_count):
    halo = np.concatenate([np.arange(-BIN_HALF, 0), np.arange(bin_count, bin_count + BIN_HALF)])
    own = np.arange(bin_count).reshape(-1, 1, PACK)
    parts = np.arange(2).reshape(1, 2, 1)
    shape = (bin_count // PACK, 2, PACK)
    bins = np.concatenate([halo, halo, np.broadcast_to(own, shape).ravel()])
    part = np.concatenate(
        [np.zeros_like(halo), np.ones_like(halo), np.broadcast_to(parts, shape).ravel()]
    )
    return bins, part


def dft_tables(freq_devices, samples):
    bin_count = BINS // freq_devices
    bins, part = bin_columns(bin_count)
    sample_ids = np.arange(samples)
    tables = []
    for device in range(freq_devices):
        freq = device * bin_count + bins + 1
        inside = (freq >= 1) & (freq <= BINS)
        turn = (freq[None, :] * sample_ids[:, None]) % samples
        phase = turn.astype(np.float32) * np.float32(2.0 * math.pi / samples)
        wave = np.where(part[None, :] == 0, np.cos(phase), -np.sin(phase)).astype(np.float32)
        wave = wave * np.float32(1.0 / math.sqrt(samples)) * inside[None, :]
        tables.append(wave.astype(ml_dtypes.bfloat16))
    return np.stack(tables)


def smoother(bin_count):
    bins, _ = bin_columns(bin_count)
    own = bins[4 * BIN_HALF :]
    return (np.abs(bins[:, None] - own[None, :]) <= BIN_HALF).astype(ml_dtypes.bfloat16)


def whiten_kernel(
    x_hbm, ok_hbm, win_hbm, table_hbm, smooth_hbm, out_ref,
    x_ref, ok_ref, win_ref, table_ref, smooth_ref, mag_ref, level_ref, spec_ref, x_sems, table_sems, sems,
):
    channels, windows, samples = x_ref.shape
    rows = channels * windows
    halo = 4 * BIN_HALF
    own = table_ref.shape[1] - halo
    tile = 2 * TIME_HALF
    count = 2 * TIME_HALF + 1
    tiles = samples // tile
    q = lax.axis_index("freq")

    def chunk(k):
        return pl.ds(k * CHUNK, CHUNK)

    x_copies = [
        pltpu.make_async_copy(x_hbm.at[:, :, chunk(k)], x_ref.at[:, :, chunk(k)], x_sems.at[k])
        for k in range(samples // CHUNK)
    ]
    table_copies = [
        pltpu.make_async_copy(table_hbm.at[q, chunk(k)], table_ref.at[chunk(k)], table_sems.at[k])
        for k in range(samples // CHUNK)
    ]
    small_copies = [
        pltpu.make_async_copy(source, target, sems.at[k])
        for k, (source, target) in enumerate(
            ((ok_hbm, ok_ref), (win_hbm, win_ref), (smooth_hbm, smooth_ref))
        )
    ]
    for copy in x_copies + table_copies + small_copies:
        copy.start()

    mag_ref[:, :TIME_HALF] = jnp.zeros((rows, TIME_HALF), jnp.bfloat16)
    mag_ref[:, TIME_HALF + samples :] = jnp.zeros((rows, TIME_HALF), jnp.bfloat16)
    source = lax.broadcasted_iota(jnp.int32, (2 * tile, tile), 0) - TIME_HALF
    target = lax.broadcasted_iota(jnp.int32, (2 * tile, tile), 1)
    band = (jnp.abs(source - target) <= TIME_HALF).astype(jnp.float32).astype(jnp.bfloat16)

    def loaded(t):
        return x_ref[:, :, t * tile : (t + 1) * tile].astype(jnp.float32).reshape(rows, tile)

    for t in range(tiles):
        if t * tile % CHUNK == 0:
            x_copies[t * tile // CHUNK].wait()
        mag_ref[:, TIME_HALF + t * tile : TIME_HALF + (t + 1) * tile] = jnp.abs(loaded(t)).astype(
            jnp.bfloat16
        )
    for t in range(tiles):
        sums = jnp.dot(
            mag_ref[:, t * tile : (t + 2) * tile], band, preferred_element_type=jnp.float32
        )
        level_ref[:, t * tile : (t + 1) * tile] = (
            loaded(t) * (count / (sums + count * 1e-06))
        ).astype(jnp.bfloat16)
    for copy in table_copies + small_copies:
        copy.wait()
    flags = (ok_ref[...] * win_ref[...]).astype(jnp.float32).astype(jnp.bfloat16)
    lane = lax.broadcasted_iota(jnp.int32, (windows, LANES), 1)
    window = lax.broadcasted_iota(jnp.int32, (windows, LANES), 0)
    contract = (((0,), (0,)), ((), ()))
    picked = (lane == window).astype(jnp.float32).astype(jnp.bfloat16)
    out_ref[:, windows * own :] = lax.dot_general(
        flags, picked, contract, preferred_element_type=jnp.float32
    ).astype(jnp.bfloat16)
    width = 2 * PACK
    usable = []
    for g in range(LANES // width):
        spread = (lax.rem(lane // width + windows - g, windows) == window).astype(jnp.float32)
        usable.append(
            lax.dot_general(
                flags, spread.astype(jnp.bfloat16), contract, preferred_element_type=jnp.float32
            )
        )

    ones = smooth_ref[...]
    half = channels // HALVES
    block = lax.broadcasted_iota(jnp.int32, (half, LANES), 1) // width
    for h in range(HALVES):
        part = slice(h * half * windows, (h + 1) * half * windows)
        spectra = jnp.dot(level_ref[part], table_ref[...], preferred_element_type=jnp.float32)
        power = spectra * spectra
        smooth = jnp.dot(power.astype(jnp.bfloat16), ones, preferred_element_type=jnp.float32)
        white = spectra[:, halo:] * lax.rsqrt(smooth * (1.0 / (2 * BIN_HALF + 1)) + 1e-06)
        for t in range(0, own, LANES):
            tile_width = min(LANES, own - t)
            tile_white = white[:, t : t + tile_width]
            if tile_width < LANES:
                rest = jnp.zeros((half * windows, LANES - tile_width), jnp.float32)
                tile_white = jnp.concatenate([tile_white, rest], axis=1)
            turned = pltpu.roll(tile_white, 0, 1, stride=width, stride_axis=0)
            spec_ref[h, t // LANES] = turned
            windows_of = [spec_ref[h, t // LANES, pl.ds(w, half, stride=windows), :] for w in range(windows)]
            for g in range(tile_width // width):
                packed = windows_of[0]
                for w in range(1, windows):
                    packed = jnp.where(block == (g + w) % windows, windows_of[w], packed)
                packed = packed * usable[g][h * half : (h + 1) * half]
                at = (t // width + g) * LANES
                out_ref[h * half : (h + 1) * half, at : at + LANES] = packed.astype(jnp.bfloat16)


def whiten(strain, channel_ok, window_ok, freq_devices):
    channels, windows, samples = strain.shape
    bin_count = BINS // freq_devices
    tables = jnp.asarray(dft_tables(freq_devices, samples))
    ones = jnp.asarray(smoother(bin_count))
    columns = tables.shape[2]
    own = 2 * bin_count
    rows = channels * windows
    chunks = samples // CHUNK
    return pl.pallas_call(
        whiten_kernel,
        in_specs=[pl.BlockSpec(memory_space=pltpu.HBM)] * 5,
        out_specs=pl.BlockSpec(memory_space=pltpu.VMEM),
        out_shape=pltpu.VMEM((channels, windows * own + LANES), jnp.bfloat16),
        scratch_shapes=[
            pltpu.VMEM((channels, windows, samples), jnp.bfloat16),
            pltpu.VMEM((1, channels), jnp.int32),
            pltpu.VMEM((windows, channels), jnp.int32),
            pltpu.VMEM((samples, columns), jnp.bfloat16),
            pltpu.VMEM((columns, own), jnp.bfloat16),
            pltpu.VMEM((rows, samples + 2 * TIME_HALF), jnp.bfloat16),
            pltpu.VMEM((rows, samples), jnp.bfloat16),
            pltpu.VMEM((HALVES, -(-own // LANES), rows // HALVES, LANES), jnp.float32),
            pltpu.SemaphoreType.DMA((chunks,)),
            pltpu.SemaphoreType.DMA((chunks,)),
            pltpu.SemaphoreType.DMA((3,)),
        ],
        compiler_params=pltpu.CompilerParams(vmem_limit_bytes=VMEM_BYTES),
        name="whiten",
    )(
        *(
            pltpu.with_memory_space_constraint(value, pltpu.HBM)
            for value in (strain, channel_ok.reshape(1, channels), window_ok.T, tables, ones)
        )
    )


def trade(value, partner):
    count = lax.axis_size("ch")
    inside = lambda i: 0 <= partner(i) < count
    return lax.ppermute(value, "ch", [(i, partner(i) if inside(i) else beside(i)) for i in range(count)])


def beside(i):
    return i + 1 - 2 * (i % 2)


def partner_pair(i):
    return i + 2 - 4 * (i // 2 % 2)


def other_pair(i):
    return i - 2 + 4 * (i // 2 % 2)


def partner_far(i):
    return i + 4 - 8 * (i // 4 % 2)


def other_far(i):
    return i - 4 + 8 * (i // 4 % 2)


SHARE = (2, 0, 1)
TRADES = (partner_pair, other_pair, partner_far, other_far)


def cross_kernel(order, own_ref, mate_ref, *refs):
    arrived, shared = [refs[order.index(k)] for k in range(4)], [refs[4 + SHARE.index(k)] for k in range(3)]
    (ahead_hbm, behind_hbm, partners_ref, div_ahead, div_behind, count_ref, *products) = refs[7:-3]
    ahead_ref, behind_ref, sems = refs[-3:]
    channels = own_ref.shape[0]
    packs = own_ref.shape[1] // LANES - 1
    index = lax.axis_index("ch")
    first = lax.rem(index, 2) == 0
    pair = index // 2
    near_up = lax.rem(pair, 2) == 0
    far_up = lax.rem(pair // 2, 2) == 0
    count = lax.axis_size("ch")
    met_index = [partner(index) for partner in TRADES]
    inside = [(i >= 0) & (i < count) for i in met_index]

    def neighbours(lanes):
        pick = lambda a, b: jnp.where(first, a, b)
        own, mate = own_ref[:, lanes], mate_ref[:, lanes]
        mine, theirs = [r[:, lanes] for r in arrived], [r[:, lanes] for r in shared]
        theirs.append(theirs[2])
        met = [(pick(a, b), pick(b, a)) for a, b in zip(mine, theirs, strict=True)]
        met = [tuple(jnp.where(ok, x, jnp.zeros_like(x)) for x in blocks) for ok, blocks in zip(inside, met, strict=True)]
        choose = lambda up, a, b: tuple(jnp.where(up, x, y) for x, y in zip(a, b, strict=True))
        up1, down1 = choose(near_up, met[0], met[1]), choose(near_up, met[1], met[0])
        up2, down2 = choose(far_up, met[2], met[3]), choose(far_up, met[3], met[2])
        ahead = [own, pick(mate, up1[0]), pick(up1[0], up1[1]), pick(up1[1], up2[0]), pick(up2[0], up2[1])]
        behind = [pick(down2[0], down2[1]), pick(down2[1], down1[0]), pick(down1[0], down1[1]), pick(down1[1], mate), own]
        return jnp.concatenate(ahead, axis=0), jnp.concatenate(behind, axis=0)

    total = REACH + channels
    fold = lax.broadcasted_iota(jnp.int32, (total, total), 0)
    source = lax.broadcasted_iota(jnp.int32, (total, total), 1)
    lead = 2 * channels - 1
    wanted = jnp.where(
        fold < channels,
        lead - fold,
        jnp.where(fold < REACH, REACH + lead - fold, REACH + channels - 1 - fold),
    )
    turn = (wanted == source).astype(jnp.float32).astype(jnp.bfloat16)

    def arrange(lanes):
        rows_ahead, rows_behind = neighbours(lanes)
        turned = jnp.dot(turn, rows_behind, preferred_element_type=jnp.float32).astype(jnp.bfloat16)
        partners_ref[:REACH, lanes] = rows_ahead[:REACH]
        partners_ref[REACH : 2 * REACH, lanes] = turned[:REACH]
        partners_ref[2 * REACH : 2 * REACH + channels, lanes] = rows_ahead[REACH:]
        partners_ref[2 * REACH + channels :, lanes] = turned[REACH:]

    row = lax.broadcasted_iota(jnp.int32, (channels, LANES), 0)
    lane = lax.broadcasted_iota(jnp.int32, (channels, LANES), 1)
    wrap_ahead = lane <= row
    wrap_behind = (lane >= channels) & (lane <= lead - row)
    flip = 7 - lax.broadcasted_iota(jnp.int32, (8, LANES), 0)
    part = lax.rem(lane // PACK, 2)

    def turned_rows(v):
        return jnp.take_along_axis(v, flip, axis=0)

    def skewed(ahead, behind, ends):
        a = jnp.where(wrap_ahead, ends, ahead)
        b = jnp.where(wrap_behind, ends, behind)
        aheads = []
        for r in range(0, channels, 8):
            v = pltpu.roll(turned_rows(a[r : r + 8]), (2 * LANES - r - 8) % LANES, 1, stride=1, stride_axis=0)
            aheads.append(turned_rows(v))
        b = pltpu.roll(b, LANES - 2 * channels, 1, stride=1, stride_axis=0)
        return jnp.concatenate(aheads, axis=0), b

    contract = (((1,), (1,)), ((), ()))

    def multiply(g):
        lanes = slice(g * LANES, (g + 1) * LANES)
        a = own_ref[:, lanes].astype(jnp.float32)
        rotated = jnp.where(part == 0, -pltpu.roll(a, LANES - PACK, 1), pltpu.roll(a, PACK, 1))
        zero = jnp.zeros_like(a)
        rows = []
        for f in range(PACK):
            mask = lax.rem(lane, PACK) == f
            rows += [jnp.where(mask, a, zero), jnp.where(mask, rotated, zero)]
        lhs = jnp.concatenate(rows, axis=0).astype(jnp.bfloat16)
        products[g % len(products)][:, : 2 * (REACH + channels)] = lax.dot_general(
            lhs, partners_ref[:, lanes], contract, preferred_element_type=jnp.float32
        )

    ends = sorted({1, packs - 1, packs, *range(2, packs, 2)})

    def copies(k):
        start = ends[k - 1] if k else 0
        bins = pl.ds(start * PACK, (ends[k] - start) * PACK)
        return [
            pltpu.make_async_copy(held.at[:, bins], out.at[:, bins], sems.at[q, k])
            for q, (held, out) in enumerate(((ahead_ref, ahead_hbm), (behind_ref, behind_hbm)))
        ]

    def finish(g):
        product = products[g % len(products)]
        for f in range(PACK):
            for v in range(2):
                rows = pl.ds((2 * f + v) * channels, channels)
                ahead, behind = skewed(*(product[rows, pl.ds(t * LANES, LANES)] for t in range(3)))
                ahead_ref[v, g * PACK + f] = (ahead * div_ahead[...]).astype(jnp.bfloat16)
                behind_ref[v, g * PACK + f] = (behind * div_behind[...]).astype(jnp.bfloat16)
        if g + 1 in ends:
            for copy in copies(ends.index(g + 1)):
                copy.start()

    flags = slice(packs * LANES, (packs + 1) * LANES)
    lead_packs = WIDE // LANES
    for g in range(packs):
        if g == 0:
            arrange(flags)
            count_ref[:, : 2 * (REACH + channels)] = lax.dot_general(
                own_ref[:, flags], partners_ref[:, flags], contract, preferred_element_type=jnp.float32
            )
            arrange(slice(0, WIDE))
            multiply(0)
            multiply(1)
            ahead, behind = skewed(*(count_ref[:, t * LANES : (t + 1) * LANES] for t in range(3)))
            div_ahead[...] = 1.0 / jnp.maximum(ahead, 1.0)
            div_behind[...] = 1.0 / jnp.maximum(behind, 1.0)
        at = g + lead_packs
        if at < packs and at % lead_packs == 0:
            arrange(slice(at * LANES, (at + lead_packs) * LANES))
        if g + 2 < packs:
            multiply(g + 2)
        finish(g)
    for k in range(len(ends)):
        for copy in copies(k):
            copy.wait()


def cross(values, bin_count, order):
    channels = values[0].shape[0]
    shape = jax.ShapeDtypeStruct((2, bin_count, channels, REACH), jnp.bfloat16)
    products = pltpu.VMEM((2 * PACK * channels, 3 * LANES), jnp.float32)
    held = pltpu.VMEM((2, bin_count, channels, REACH), jnp.bfloat16)
    return pl.pallas_call(
        functools.partial(cross_kernel, order),
        in_specs=[pl.BlockSpec(memory_space=pltpu.VMEM)] * len(values),
        out_specs=[pl.BlockSpec(memory_space=pl.ANY)] * 2,
        out_shape=[shape, shape],
        scratch_shapes=[
            pltpu.VMEM((2 * (REACH + channels), values[0].shape[1]), jnp.bfloat16),
            pltpu.VMEM((channels, REACH), jnp.float32),
            pltpu.VMEM((channels, REACH), jnp.float32),
            pltpu.VMEM((channels, 3 * LANES), jnp.float32),
            products,
            products,
            products,
            held,
            held,
            pltpu.SemaphoreType.DMA((2, bin_count // PACK)),
        ],
        compiler_params=pltpu.CompilerParams(vmem_limit_bytes=VMEM_BYTES),
        name="cross",
    )(*values)


def per_device(strain, channel_ok, window_ok):
    freq_devices = lax.axis_size("freq")
    own = whiten(strain, channel_ok, window_ok, freq_devices)
    mate = trade(own, beside)
    arrived = [trade(own, partner) for partner in TRADES]
    index = lax.axis_index("ch")
    ahead_first = (index // 4 + index) % 2 == 0
    shared = [trade(block, beside) for block in (*arrived[:2], jnp.where(ahead_first, arrived[2], arrived[3]))]
    order = (3, 0, 2, 1)
    last = [arrived[k] for k in order] + [shared[k] for k in SHARE]
    return cross([own, mate, *last], BINS // freq_devices, order)


def solution(mesh):
    return jax.shard_map(
        per_device,
        mesh=mesh,
        in_specs=(P("ch", None, None), P("ch"), P("ch", None)),
        out_specs=(P(None, "freq", "ch", None), P(None, "freq", "ch", None)),
        check_vma=False,
    )
```

```python
import functools
import math

import jax
import jax.numpy as jnp
import ml_dtypes
import numpy as np
from jax import lax
from jax.experimental import pallas as pl
from jax.experimental.pallas import tpu as pltpu
from jax.sharding import PartitionSpec as P

WINDOWS = 8
BINS = 256
REACH = 128
TIME_HALF = 128
BIN_HALF = 32
LANES = 128
PACK = LANES // (2 * WINDOWS)
HALVES = 1
CHUNK = 2048
WIDE = 512
VMEM_BYTES = 40 * 1024 * 1024


def bin_columns(bin_count):
    halo = np.concatenate([np.arange(-BIN_HALF, 0), np.arange(bin_count, bin_count + BIN_HALF)])
    own = np.arange(bin_count).reshape(-1, 1, PACK)
    parts = np.arange(2).reshape(1, 2, 1)
    shape = (bin_count // PACK, 2, PACK)
    bins = np.concatenate([halo, halo, np.broadcast_to(own, shape).ravel()])
    part = np.concatenate(
        [np.zeros_like(halo), np.ones_like(halo), np.broadcast_to(parts, shape).ravel()]
    )
    return bins, part


def dft_tables(freq_devices, samples):
    bin_count = BINS // freq_devices
    bins, part = bin_columns(bin_count)
    sample_ids = np.arange(samples)
    tables = []
    for device in range(freq_devices):
        freq = device * bin_count + bins + 1
        inside = (freq >= 1) & (freq <= BINS)
        turn = (freq[None, :] * sample_ids[:, None]) % samples
        phase = turn.astype(np.float32) * np.float32(2.0 * math.pi / samples)
        wave = np.where(part[None, :] == 0, np.cos(phase), -np.sin(phase)).astype(np.float32)
        wave = wave * np.float32(1.0 / math.sqrt(samples)) * inside[None, :]
        tables.append(wave.astype(ml_dtypes.bfloat16))
    return np.stack(tables)


def whiten_kernel(
    x_hbm, ok_hbm, win_hbm, table_hbm, out_ref,
    x_ref, ok_ref, win_ref, table_ref, smooth_ref, mag_ref, level_ref, spec_ref, x_sems, table_sems, sems,
):
    channels, windows, samples = x_ref.shape
    rows = channels * windows
    halo = 4 * BIN_HALF
    own = table_ref.shape[1] - halo
    tile = 2 * TIME_HALF
    count = 2 * TIME_HALF + 1
    tiles = samples // tile
    q = lax.axis_index("freq")

    def chunk(k):
        return pl.ds(k * CHUNK, CHUNK)

    x_copies = [
        pltpu.make_async_copy(x_hbm.at[:, :, chunk(k)], x_ref.at[:, :, chunk(k)], x_sems.at[k])
        for k in range(samples // CHUNK)
    ]
    table_copies = [
        pltpu.make_async_copy(table_hbm.at[q, chunk(k)], table_ref.at[chunk(k)], table_sems.at[k])
        for k in range(samples // CHUNK)
    ]
    small_copies = [
        pltpu.make_async_copy(source, target, sems.at[k])
        for k, (source, target) in enumerate(
            ((ok_hbm, ok_ref), (win_hbm, win_ref))
        )
    ]
    for copy in x_copies + table_copies + small_copies:
        copy.start()

    mag_ref[:, :TIME_HALF] = jnp.zeros((rows, TIME_HALF), jnp.bfloat16)
    mag_ref[:, TIME_HALF + samples :] = jnp.zeros((rows, TIME_HALF), jnp.bfloat16)
    source = lax.broadcasted_iota(jnp.int32, (2 * tile, tile), 0) - TIME_HALF
    target = lax.broadcasted_iota(jnp.int32, (2 * tile, tile), 1)
    band = (jnp.abs(source - target) <= TIME_HALF).astype(jnp.float32).astype(jnp.bfloat16)

    def bin_of(column):
        packed = column - halo
        beyond = lax.rem(column, 2 * BIN_HALF) - BIN_HALF
        beyond = jnp.where(beyond < 0, beyond, beyond + own // 2)
        return jnp.where(packed < 0, beyond, packed // (2 * PACK) * PACK + lax.rem(packed, PACK))

    shape = (own + halo, own)
    apart = bin_of(lax.broadcasted_iota(jnp.int32, shape, 0)) - bin_of(
        lax.broadcasted_iota(jnp.int32, shape, 1) + halo
    )
    smooth_ref[...] = (jnp.abs(apart) <= BIN_HALF).astype(jnp.float32).astype(jnp.bfloat16)

    def loaded(t):
        return x_ref[:, :, t * tile : (t + 1) * tile].astype(jnp.float32).reshape(rows, tile)

    for t in range(tiles):
        if t * tile % CHUNK == 0:
            x_copies[t * tile // CHUNK].wait()
        mag_ref[:, TIME_HALF + t * tile : TIME_HALF + (t + 1) * tile] = jnp.abs(loaded(t)).astype(
            jnp.bfloat16
        )
    for t in range(tiles):
        sums = jnp.dot(
            mag_ref[:, t * tile : (t + 2) * tile], band, preferred_element_type=jnp.float32
        )
        level_ref[:, t * tile : (t + 1) * tile] = (
            loaded(t) * (count / (sums + count * 1e-06))
        ).astype(jnp.bfloat16)
    for copy in table_copies + small_copies:
        copy.wait()
    flags = (ok_ref[...] * win_ref[...]).astype(jnp.float32).astype(jnp.bfloat16)
    lane = lax.broadcasted_iota(jnp.int32, (windows, LANES), 1)
    window = lax.broadcasted_iota(jnp.int32, (windows, LANES), 0)
    contract = (((0,), (0,)), ((), ()))
    picked = (lane == window).astype(jnp.float32).astype(jnp.bfloat16)
    out_ref[:, windows * own :] = lax.dot_general(
        flags, picked, contract, preferred_element_type=jnp.float32
    ).astype(jnp.bfloat16)
    width = 2 * PACK
    usable = []
    for g in range(LANES // width):
        spread = (lax.rem(lane // width + windows - g, windows) == window).astype(jnp.float32)
        usable.append(
            lax.dot_general(
                flags, spread.astype(jnp.bfloat16), contract, preferred_element_type=jnp.float32
            )
        )

    ones = smooth_ref[...]
    half = channels // HALVES
    block = lax.broadcasted_iota(jnp.int32, (half, LANES), 1) // width
    for h in range(HALVES):
        part = slice(h * half * windows, (h + 1) * half * windows)
        spectra = jnp.dot(level_ref[part], table_ref[...], preferred_element_type=jnp.float32)
        power = spectra * spectra
        smooth = jnp.dot(power.astype(jnp.bfloat16), ones, preferred_element_type=jnp.float32)
        white = spectra[:, halo:] * lax.rsqrt(smooth * (1.0 / (2 * BIN_HALF + 1)) + 1e-06)
        for t in range(0, own, LANES):
            tile_width = min(LANES, own - t)
            tile_white = white[:, t : t + tile_width]
            if tile_width < LANES:
                rest = jnp.zeros((half * windows, LANES - tile_width), jnp.float32)
                tile_white = jnp.concatenate([tile_white, rest], axis=1)
            turned = pltpu.roll(tile_white, 0, 1, stride=width, stride_axis=0)
            spec_ref[h, t // LANES] = turned
            windows_of = [spec_ref[h, t // LANES, pl.ds(w, half, stride=windows), :] for w in range(windows)]
            for g in range(tile_width // width):
                packed = windows_of[0]
                for w in range(1, windows):
                    packed = jnp.where(block == (g + w) % windows, windows_of[w], packed)
                packed = packed * usable[g][h * half : (h + 1) * half]
                at = (t // width + g) * LANES
                out_ref[h * half : (h + 1) * half, at : at + LANES] = packed.astype(jnp.bfloat16)


def whiten(strain, channel_ok, window_ok, freq_devices):
    channels, windows, samples = strain.shape
    bin_count = BINS // freq_devices
    tables = jnp.asarray(dft_tables(freq_devices, samples))
    columns = tables.shape[2]
    own = 2 * bin_count
    rows = channels * windows
    chunks = samples // CHUNK
    return pl.pallas_call(
        whiten_kernel,
        in_specs=[pl.BlockSpec(memory_space=pltpu.HBM)] * 4,
        out_specs=pl.BlockSpec(memory_space=pltpu.VMEM),
        out_shape=pltpu.VMEM((channels, windows * own + LANES), jnp.bfloat16),
        scratch_shapes=[
            pltpu.VMEM((channels, windows, samples), jnp.bfloat16),
            pltpu.VMEM((1, channels), jnp.int32),
            pltpu.VMEM((windows, channels), jnp.int32),
            pltpu.VMEM((samples, columns), jnp.bfloat16),
            pltpu.VMEM((columns, own), jnp.bfloat16),
            pltpu.VMEM((rows, samples + 2 * TIME_HALF), jnp.bfloat16),
            pltpu.VMEM((rows, samples), jnp.bfloat16),
            pltpu.VMEM((HALVES, -(-own // LANES), rows // HALVES, LANES), jnp.float32),
            pltpu.SemaphoreType.DMA((chunks,)),
            pltpu.SemaphoreType.DMA((chunks,)),
            pltpu.SemaphoreType.DMA((2,)),
        ],
        compiler_params=pltpu.CompilerParams(vmem_limit_bytes=VMEM_BYTES),
        name="whiten",
    )(
        *(
            pltpu.with_memory_space_constraint(value, pltpu.HBM)
            for value in (strain, channel_ok.reshape(1, channels), window_ok.T, tables)
        )
    )


def trade(value, partner):
    count = lax.axis_size("ch")
    inside = lambda i: 0 <= partner(i) < count
    return lax.ppermute(value, "ch", [(i, partner(i) if inside(i) else beside(i)) for i in range(count)])


def beside(i):
    return i + 1 - 2 * (i % 2)


def partner_pair(i):
    return i + 2 - 4 * (i // 2 % 2)


def other_pair(i):
    return i - 2 + 4 * (i // 2 % 2)


def partner_far(i):
    return i + 4 - 8 * (i // 4 % 2)


def other_far(i):
    return i - 4 + 8 * (i // 4 % 2)


SHARE = (2, 0, 1)
TRADES = (partner_pair, other_pair, partner_far, other_far)


def cross_kernel(order, own_ref, mate_ref, *refs):
    arrived, shared = [refs[order.index(k)] for k in range(4)], [refs[4 + SHARE.index(k)] for k in range(3)]
    (ahead_hbm, behind_hbm, partners_ref, div_ahead, div_behind, count_ref, *products) = refs[7:-3]
    ahead_ref, behind_ref, sems = refs[-3:]
    channels = own_ref.shape[0]
    packs = own_ref.shape[1] // LANES - 1
    index = lax.axis_index("ch")
    first = lax.rem(index, 2) == 0
    pair = index // 2
    near_up = lax.rem(pair, 2) == 0
    far_up = lax.rem(pair // 2, 2) == 0
    count = lax.axis_size("ch")
    met_index = [partner(index) for partner in TRADES]
    inside = [(i >= 0) & (i < count) for i in met_index]

    def neighbours(lanes):
        pick = lambda a, b: jnp.where(first, a, b)
        own, mate = own_ref[:, lanes], mate_ref[:, lanes]
        mine, theirs = [r[:, lanes] for r in arrived], [r[:, lanes] for r in shared]
        theirs.append(theirs[2])
        met = [(pick(a, b), pick(b, a)) for a, b in zip(mine, theirs, strict=True)]
        met = [tuple(jnp.where(ok, x, jnp.zeros_like(x)) for x in blocks) for ok, blocks in zip(inside, met, strict=True)]
        choose = lambda up, a, b: tuple(jnp.where(up, x, y) for x, y in zip(a, b, strict=True))
        up1, down1 = choose(near_up, met[0], met[1]), choose(near_up, met[1], met[0])
        up2, down2 = choose(far_up, met[2], met[3]), choose(far_up, met[3], met[2])
        ahead = [own, pick(mate, up1[0]), pick(up1[0], up1[1]), pick(up1[1], up2[0]), pick(up2[0], up2[1])]
        behind = [pick(down2[0], down2[1]), pick(down2[1], down1[0]), pick(down1[0], down1[1]), pick(down1[1], mate), own]
        return jnp.concatenate(ahead, axis=0), jnp.concatenate(behind, axis=0)

    total = REACH + channels
    fold = lax.broadcasted_iota(jnp.int32, (total, total), 0)
    source = lax.broadcasted_iota(jnp.int32, (total, total), 1)
    lead = 2 * channels - 1
    wanted = jnp.where(
        fold < channels,
        lead - fold,
        jnp.where(fold < REACH, REACH + lead - fold, REACH + channels - 1 - fold),
    )
    turn = (wanted == source).astype(jnp.float32).astype(jnp.bfloat16)

    def arrange(lanes):
        rows_ahead, rows_behind = neighbours(lanes)
        turned = jnp.dot(turn, rows_behind, preferred_element_type=jnp.float32).astype(jnp.bfloat16)
        partners_ref[:REACH, lanes] = rows_ahead[:REACH]
        partners_ref[REACH : 2 * REACH, lanes] = turned[:REACH]
        partners_ref[2 * REACH : 2 * REACH + channels, lanes] = rows_ahead[REACH:]
        partners_ref[2 * REACH + channels :, lanes] = turned[REACH:]

    row = lax.broadcasted_iota(jnp.int32, (channels, LANES), 0)
    lane = lax.broadcasted_iota(jnp.int32, (channels, LANES), 1)
    wrap_ahead = lane <= row
    wrap_behind = (lane >= channels) & (lane <= lead - row)
    flip = 7 - lax.broadcasted_iota(jnp.int32, (8, LANES), 0)
    part = lax.rem(lane // PACK, 2)

    def turned_rows(v):
        return jnp.take_along_axis(v, flip, axis=0)

    def skewed(ahead, behind, ends):
        a = jnp.where(wrap_ahead, ends, ahead)
        b = jnp.where(wrap_behind, ends, behind)
        aheads = []
        for r in range(0, channels, 8):
            v = pltpu.roll(turned_rows(a[r : r + 8]), (2 * LANES - r - 8) % LANES, 1, stride=1, stride_axis=0)
            aheads.append(turned_rows(v))
        b = pltpu.roll(b, LANES - 2 * channels, 1, stride=1, stride_axis=0)
        return jnp.concatenate(aheads, axis=0), b

    contract = (((1,), (1,)), ((), ()))

    def multiply(g):
        lanes = slice(g * LANES, (g + 1) * LANES)
        a = own_ref[:, lanes].astype(jnp.float32)
        rotated = jnp.where(part == 0, -pltpu.roll(a, LANES - PACK, 1), pltpu.roll(a, PACK, 1))
        zero = jnp.zeros_like(a)
        rows = []
        for f in range(PACK):
            mask = lax.rem(lane, PACK) == f
            rows += [jnp.where(mask, a, zero), jnp.where(mask, rotated, zero)]
        lhs = jnp.concatenate(rows, axis=0).astype(jnp.bfloat16)
        products[g % len(products)][:, : 2 * (REACH + channels)] = lax.dot_general(
            lhs, partners_ref[:, lanes], contract, preferred_element_type=jnp.float32
        )

    ends = sorted({1, packs - 1, packs, *range(2, packs, 2)})

    def copies(k):
        start = ends[k - 1] if k else 0
        bins = pl.ds(start * PACK, (ends[k] - start) * PACK)
        return [
            pltpu.make_async_copy(held.at[:, bins], out.at[:, bins], sems.at[q, k])
            for q, (held, out) in enumerate(((ahead_ref, ahead_hbm), (behind_ref, behind_hbm)))
        ]

    def finish(g):
        product = products[g % len(products)]
        for f in range(PACK):
            for v in range(2):
                rows = pl.ds((2 * f + v) * channels, channels)
                ahead, behind = skewed(*(product[rows, pl.ds(t * LANES, LANES)] for t in range(3)))
                ahead_ref[v, g * PACK + f] = (ahead * div_ahead[...]).astype(jnp.bfloat16)
                behind_ref[v, g * PACK + f] = (behind * div_behind[...]).astype(jnp.bfloat16)
        if g + 1 in ends:
            for copy in copies(ends.index(g + 1)):
                copy.start()

    flags = slice(packs * LANES, (packs + 1) * LANES)
    lead_packs = WIDE // LANES
    for g in range(packs):
        if g == 0:
            arrange(flags)
            count_ref[:, : 2 * (REACH + channels)] = lax.dot_general(
                own_ref[:, flags], partners_ref[:, flags], contract, preferred_element_type=jnp.float32
            )
            arrange(slice(0, WIDE))
            multiply(0)
            multiply(1)
            ahead, behind = skewed(*(count_ref[:, t * LANES : (t + 1) * LANES] for t in range(3)))
            div_ahead[...] = 1.0 / jnp.maximum(ahead, 1.0)
            div_behind[...] = 1.0 / jnp.maximum(behind, 1.0)
        at = g + lead_packs
        if at < packs and at % lead_packs == 0:
            arrange(slice(at * LANES, (at + lead_packs) * LANES))
        if g + 2 < packs:
            multiply(g + 2)
        finish(g)
    for k in range(len(ends)):
        for copy in copies(k):
            copy.wait()


def cross(values, bin_count, order):
    channels = values[0].shape[0]
    shape = jax.ShapeDtypeStruct((2, bin_count, channels, REACH), jnp.bfloat16)
    products = pltpu.VMEM((2 * PACK * channels, 3 * LANES), jnp.float32)
    held = pltpu.VMEM((2, bin_count, channels, REACH), jnp.bfloat16)
    return pl.pallas_call(
        functools.partial(cross_kernel, order),
        in_specs=[pl.BlockSpec(memory_space=pltpu.VMEM)] * len(values),
        out_specs=[pl.BlockSpec(memory_space=pl.ANY)] * 2,
        out_shape=[shape, shape],
        scratch_shapes=[
            pltpu.VMEM((2 * (REACH + channels), values[0].shape[1]), jnp.bfloat16),
            pltpu.VMEM((channels, REACH), jnp.float32),
            pltpu.VMEM((channels, REACH), jnp.float32),
            pltpu.VMEM((channels, 3 * LANES), jnp.float32),
            products,
            products,
            products,
            held,
            held,
            pltpu.SemaphoreType.DMA((2, bin_count // PACK)),
        ],
        compiler_params=pltpu.CompilerParams(vmem_limit_bytes=VMEM_BYTES),
        name="cross",
    )(*values)


def per_device(strain, channel_ok, window_ok):
    freq_devices = lax.axis_size("freq")
    own = whiten(strain, channel_ok, window_ok, freq_devices)
    mate = trade(own, beside)
    arrived = [trade(own, partner) for partner in TRADES]
    index = lax.axis_index("ch")
    ahead_first = (index // 4 + index) % 2 == 0
    shared = [trade(block, beside) for block in (*arrived[:2], jnp.where(ahead_first, arrived[2], arrived[3]))]
    order = (3, 0, 2, 1)
    last = [arrived[k] for k in order] + [shared[k] for k in SHARE]
    return cross([own, mate, *last], BINS // freq_devices, order)


def solution(mesh):
    return jax.shard_map(
        per_device,
        mesh=mesh,
        in_specs=(P("ch", None, None), P("ch"), P("ch", None)),
        out_specs=(P(None, "freq", "ch", None), P(None, "freq", "ch", None)),
        check_vma=False,
    )
```
